32 devices in a mesh: frame: 8 (over z, x), head: 4 (over y, core).
Axes of the slice: x: 2, y: 2, z: 4, core: 2. Of those that a mesh axis runs over, the one named last changes fastest.
Arguments:
- queries: bfloat16 [16, 8, 32, 896], P('frame', None, None, 'head'), may hold values from -6 to 6
- key_vectors: bfloat16 [16, 8, 32, 896], P('frame', None, None, 'head'), may hold values from -6 to 6
- value_vectors: bfloat16 [16, 8, 32, 896], P('frame', None, None, 'head'), may hold values from -8 to 8
- frame_index: int32 [16], P('frame'), may hold values from 0 to 31, as said below
- height_index: int32 [8], replicated, may hold values from 0 to 15, as said below
- width_index: int32 [32], replicated, may hold values from 0 to 63, as said below
- frame_block: int32 [16], P('frame'), may hold values from 0 to 4, never falling along the last dimension, each value on 1 to 6 neighbouring positions
- conv_weight: bfloat16 [3, 896, 2240], P(None, 'head'), may hold values from -0.125 to 0.125
- conv_bias: float32 [2240], replicated, may hold values from -0.8 to 0.8
Outputs:
- mixed_frames: bfloat16 [8, 16, 32, 2240], P('head', 'frame')
The draws below stay inside these ranges and needn't reach their ends.
Inputs may be any that keep to these rules, and one draw needn't show every extreme that they name: `frame_index`: strictly increasing over the frames, first entry 0, last entry 31. `height_index`: strictly increasing over the rows, first entry 0, last entry 15. `width_index`: strictly increasing over the columns, first entry 0, last entry 63.
All inputs are finite; a program needn't handle non-finite values.
Results may differ from the reference program's by a relative error of at most 0.0043.
The reference program's roundings to bfloat16 on the way (of `attended`) count: a program that leaves them out, or rounds other values in their place, can miss the bound.
Values may be sent and summed in bfloat16 or wider, within the bound.
A program may use at most 128 MiB of HBM per device.

```python
import math
import jax
import jax.numpy as jnp
import numpy as np
from jax import lax

HD = 112
HEADS_DEV = 2
CHANNELS = 896
C_OUT = 2240
FRAMES = 16
HGT = 8
WID = 32
N_HEAD = 4


def rising_positions(key, salt, length):
    inner_key = jax.random.fold_in(key, salt)
    chosen = jax.random.permutation(inner_key, 2 * length - 2)[:length - 2] + 1
    middle = jnp.sort(chosen.astype(jnp.int32))
    first = jnp.zeros((1,), jnp.int32)
    last = jnp.full((1,), 2 * length - 1, jnp.int32)
    return jnp.concatenate([first, middle, last]).astype(jnp.int32)


def draw_frame_index(key, part):
    return rising_positions(key, 11, FRAMES)


def draw_height_index(key, part):
    return rising_positions(key, 12, HGT)


def draw_width_index(key, part):
    return rising_positions(key, 13, WID)


def draw_value_vectors(key, part):
    base_key = jax.random.fold_in(key, 21)
    common_key, slope_key, frame_key, noise_key = jax.random.split(base_key, 4)
    common = jax.random.normal(common_key, (CHANNELS,), jnp.float32)
    slope = jax.random.normal(slope_key, (CHANNELS,), jnp.float32)
    frame_part = jax.random.normal(frame_key, (FRAMES, 1, 1, CHANNELS), jnp.float32)
    ramp = (2.0 * jnp.arange(FRAMES, dtype=jnp.float32) / max(FRAMES - 1, 1) - 1.0).reshape(FRAMES, 1, 1, 1)
    noise = jax.random.normal(noise_key, (FRAMES, HGT, WID, CHANNELS), jnp.float32)
    mean_part = 0.7 * common + 0.7 * slope * ramp + 0.4 * frame_part
    return jnp.clip(mean_part + noise, -8.0, 8.0).astype(jnp.bfloat16)


def steps_of(own_key, extent, shards, least, largest):
    level, own = 1.0, jax.random.fold_in(own_key, 6)
    for dim, blocks in shards:
        steps = jnp.exp(jax.random.uniform(jax.random.fold_in(own, dim), (blocks,), jnp.float32, least / len(shards), largest / len(shards)))
        level = level * jnp.repeat(steps, extent[dim] // blocks).reshape([-1 if axis == dim else 1 for axis in range(len(extent))])
    return level


def split_up(number_of, total, limit, skew):
    portions = [(1 << 20) // math.isqrt(grade ** skew) + 1 for grade in range(2, number_of + 1)]
    surplus, holding = total - limit - (number_of - 1), [1] * (number_of - 1)
    while surplus > 0:
        candidates = [i for i in range(number_of - 1) if holding[i] < limit]
        whole, remaining = sum([portions[i] for i in candidates]), surplus
        for i in candidates:
            extra = min(limit - holding[i], max(1, remaining * portions[i] // whole), surplus)
            holding[i] = holding[i] + extra
            surplus = surplus - extra
    return np.array([limit] + holding)


def ragged(key, count, total, bound, skew):
    if count == 2:
        one = jax.random.randint(key, (), max(1, total - bound), min(bound, total - 1) + 1)
        return jnp.stack([one, total - one])
    sizes = jnp.asarray(split_up(count, total, bound, skew), jnp.int32)
    couples = (count - 1) // 2
    giver, taker = sizes[1:1 + 2 * couples:2], sizes[2:2 + 2 * couples:2]
    margin = jnp.minimum(giver - 1, bound - taker)
    moved = jax.random.randint(jax.random.fold_in(key, 1), (couples,), 0, 1 << 20) % (margin + 1)
    sizes = sizes.at[1:1 + 2 * couples:2].set(giver - moved).at[2:2 + 2 * couples:2].set(taker + moved)
    return sizes[jax.random.permutation(jax.random.fold_in(key, 2), count)]


def centred(stream_key, shape, spread, limit, cuts=(), kind=jnp.bfloat16):
    factor_of = steps_of(stream_key, shape, cuts, -0.22, 0.18) if cuts else 1.0
    result = jax.random.normal(stream_key, shape, jnp.float32) * spread * factor_of
    return jnp.minimum(jnp.maximum(result, -limit), limit).astype(kind)


def setup_inputs(seed: int = 0) -> dict:
    key_of = jax.random.split(jax.random.key(seed), 10)
    queries = centred(key_of[0], (FRAMES, HGT, WID, CHANNELS), 1.0, 6.0, ((0, 8), (3, 4)))
    key_vectors = centred(key_of[1], (FRAMES, HGT, WID, CHANNELS), 1.0, 6.0, ((0, 8), (3, 4)))
    value_vectors = draw_value_vectors(jax.random.fold_in(key_of[9], 71), 0)
    frame_index = draw_frame_index(jax.random.fold_in(key_of[9], 71), 0)
    height_index = draw_height_index(jax.random.fold_in(key_of[9], 71), 0)
    width_index = draw_width_index(jax.random.fold_in(key_of[9], 71), 0)
    frame_block = jnp.searchsorted(jnp.cumsum(ragged(key_of[6], FRAMES // 3, FRAMES, 6, 1)), jnp.arange(FRAMES), side="right").astype(jnp.int32)
    conv_weight = centred(key_of[7], (3, CHANNELS, C_OUT), (3 * CHANNELS) ** -0.5, 0.125, ((1, 4),))
    conv_bias = centred(key_of[8], (C_OUT,), 0.2, 0.8, (), jnp.float32)
    return {"queries": queries, "key_vectors": key_vectors, "value_vectors": value_vectors, "frame_index": frame_index, "height_index": height_index, "width_index": width_index, "frame_block": frame_block, "conv_weight": conv_weight, "conv_bias": conv_bias}


EPSILON = 1e-6
HIGHEST = lax.Precision.HIGHEST


def spin_part(section, positions, axis_slot):
    half_size = section.shape[-1] // 2
    inverse = 10000.0 ** (-2.0 * jnp.arange(half_size, dtype=jnp.float32) / section.shape[-1])
    angles = positions.astype(jnp.float32)[:, None] * inverse[None, :]
    target = [1, 1, 1, 1, half_size]
    target[axis_slot] = positions.shape[0]
    angles = angles.reshape(target)
    cosine = jnp.cos(angles)
    sine_values = jnp.sin(angles)
    lower_half = section[..., :half_size]
    upper_half = section[..., half_size:]
    return jnp.concatenate([lower_half * cosine - upper_half * sine_values, upper_half * cosine + lower_half * sine_values], axis=-1)


def rotate(values, frame_pos, height_pos, width_pos):
    head_size = values.shape[-1]
    side_size = (head_size * 5 // 14) // 2 * 2
    first_size = head_size - 2 * side_size
    return jnp.concatenate([
        spin_part(values[..., :first_size], frame_pos, 0),
        spin_part(values[..., first_size:first_size + side_size], height_pos, 1),
        spin_part(values[..., first_size + side_size:], width_pos, 2)], axis=-1)


def reference(queries, key_vectors, value_vectors, frame_index, height_index, width_index, frame_block, conv_weight, conv_bias):
    group_width = HEADS_DEV * HD
    split_shape = (FRAMES, HGT, WID, HEADS_DEV, HD)
    allowed = (frame_block[None, :] <= frame_block[:, None]).astype(jnp.float32)
    summed = jnp.zeros((FRAMES, HGT, WID, C_OUT), jnp.float32)
    for group_index in range(N_HEAD):
        columns = slice(group_index * group_width, (group_index + 1) * group_width)
        query_pos = jax.nn.relu(queries[..., columns].astype(jnp.float32)).reshape(split_shape)
        key_pos = jax.nn.relu(key_vectors[..., columns].astype(jnp.float32)).reshape(split_shape)
        value_rows = value_vectors[..., columns].astype(jnp.float32).reshape(split_shape)
        query_rot = rotate(query_pos, frame_index, height_index, width_index)
        key_rot = rotate(key_pos, frame_index, height_index, width_index)
        frame_states = jnp.einsum('fyxhd,fyxhe->fhde', key_rot, value_rows, precision=HIGHEST)
        frame_sums = jnp.sum(key_pos, axis=(1, 2))
        states = jnp.einsum('tf,fhde->thde', allowed, frame_states, precision=HIGHEST)
        key_totals = jnp.einsum('tf,fhd->thd', allowed, frame_sums, precision=HIGHEST)
        numerator = jnp.einsum('tyxhd,thde->tyxhe', query_rot, states, precision=HIGHEST)
        denominator = jnp.einsum('tyxhd,thd->tyxh', query_pos, key_totals, precision=HIGHEST) + EPSILON
        attended = (numerator / denominator[..., None]).astype(jnp.bfloat16).reshape(FRAMES, HGT, WID, group_width)
        padded = jnp.concatenate([jnp.zeros((2, HGT, WID, group_width), jnp.bfloat16), attended], axis=0)
        for tap_index in range(3):
            shifted = padded[2 - tap_index:2 - tap_index + FRAMES].reshape(-1, group_width)
            product = jnp.dot(shifted, conv_weight[tap_index, columns], preferred_element_type=jnp.float32)
            summed = summed + product.reshape(FRAMES, HGT, WID, C_OUT)
    activated = jax.nn.silu(summed + conv_bias).astype(jnp.bfloat16)
    return jnp.transpose(activated, (1, 0, 2, 3))
```

```python
import functools

import jax
import jax.numpy as jnp
import numpy as np
from jax import lax
from jax.experimental import pallas as pl
from jax.experimental.pallas import tpu as pltpu
from jax.sharding import PartitionSpec as P

HD = 112
PAD = 128
EPSILON = 1e-06
BLOCK_MOST = 6
COLUMNS = 512
F32 = jnp.float32
BF16 = jnp.bfloat16


def sections():
    side = HD * 5 // 14 // 2 * 2
    first = HD - 2 * side
    return ((0, first), (first, side), (first + side, side))


def tables(heads):
    spread = np.zeros((heads * HD, heads * PAD), np.float32)
    swap = np.zeros((heads * HD, heads * PAD), np.float32)
    freq = np.zeros((8, heads * PAD), np.float32)
    for h in range(heads):
        for j in range(HD):
            spread[h * HD + j, h * PAD + j] = 1.0
        for s, (start, n) in enumerate(sections()):
            half = n // 2
            for j in range(half):
                a, b = start + j, start + half + j
                swap[h * HD + b, h * PAD + a] = -1.0
                swap[h * HD + a, h * PAD + b] = 1.0
                for d in (a, b):
                    freq[s, h * PAD + d] = 10000.0 ** (-2.0 * j / n)
                    freq[3 + s, h * PAD + d] = 1.0
    return spread, swap, freq


def mm(a, b):
    return jnp.dot(a, b, preferred_element_type=F32)


def mm_t(a, b):
    return lax.dot_general(a, b, (((0,), (0,)), ((), ())), preferred_element_type=F32)


def split(a):
    high = a.astype(BF16)
    return high, (a - high.astype(F32)).astype(BF16)


def kernel(
    cfg, fb_ref, q_ref, k_ref, v_ref, pos_ref, freq_ref, spread_ref, swap_ref, gather_ref, w_ref, bias_ref, out_ref,
    w_buf, qh, time_own, time_prev, msg_t, msg_l, recv_t, recv_l, recv_p, state, att, att_x, *rest,
):
    F, Y, heads, HG, W, chunks = cfg
    n_chunk = len(chunks)
    part_send, part_recv, part_own = rest[:n_chunk], rest[n_chunk : 2 * n_chunk], rest[2 * n_chunk : 3 * n_chunk]
    (w_sem, w_send, w_recv, halo_send, halo_recv, t_send, t_recv, l_send, l_recv, p_send, p_recv,
     x_send, x_recv, c_send, c_recv) = rest[3 * n_chunk :]
    FC = 2
    H = 2 * Y
    TF = HG * W
    RD = HG // H
    TD = RD * W
    reach = min(F - 1, -(-(BLOCK_MOST - 1) // FC))
    f = lax.axis_index("frame")
    h = lax.axis_index("head")
    y, c = h // 2, h % 2
    mate = 2 * y + (1 - c)

    barrier = pltpu.get_barrier_semaphore()
    for k in range(1, F):
        pl.semaphore_signal(barrier, inc=1, device_id=(lax.rem(f + k, F), h), device_id_type=pl.DeviceIdType.MESH)
    pl.semaphore_signal(barrier, inc=1, device_id=(f, mate), device_id_type=pl.DeviceIdType.MESH)
    for j in range(1, Y):
        pl.semaphore_signal(
            barrier, inc=1, device_id=(f, 2 * lax.rem(y + j, Y) + c), device_id_type=pl.DeviceIdType.MESH
        )

    def remote(src, dst, send, recv, frame, head):
        return pltpu.make_async_remote_copy(
            src_ref=src, dst_ref=dst, send_sem=send, recv_sem=recv,
            device_id=(frame, head), device_id_type=pl.DeviceIdType.MESH,
        )

    w_local = pltpu.make_async_copy(w_ref, w_buf.at[0], w_sem)
    w_local.start()

    width = pos_ref[0:W, :]
    height = pos_ref[W : W + HG, :]
    times = pos_ref[W + HG : W + HG + 8, :]
    freq = freq_ref[...]
    t_ang = times * freq[0:1]
    time_own[0:8, :] = jnp.cos(t_ang) * freq[3:4]
    time_own[8:16, :] = jnp.sin(t_ang)
    h_ang = height * freq[1:2]
    w_ang = width * freq[2:3]
    lanes = heads * PAD
    cos_hw = (
        (jnp.cos(h_ang) * freq[4:5]).reshape(HG, 1, lanes) + (jnp.cos(w_ang) * freq[5:6]).reshape(1, W, lanes)
    ).reshape(TF, lanes)
    sin_hw = (jnp.sin(h_ang).reshape(HG, 1, lanes) + jnp.sin(w_ang).reshape(1, W, lanes)).reshape(TF, lanes)

    pl.semaphore_wait(barrier, (F - 1) + 1 + (Y - 1))

    w_far = remote(w_ref, w_buf.at[1], w_send, w_recv, f, mate)
    w_far.start()
    nxt = lax.rem(f + 1, F)
    q_copy = remote(q_ref, qh, halo_send.at[0], halo_recv.at[0], nxt, h)
    t_copy = remote(time_own, time_prev, halo_send.at[1], halo_recv.at[1], nxt, h)

    @pl.when(f < F - 1)
    def _():
        q_copy.start()
        t_copy.start()

    @pl.when(f == 0)
    def _():
        qh[...] = jnp.zeros_like(qh)
        time_prev[...] = jnp.zeros_like(time_prev)
        recv_t[0] = jnp.zeros_like(recv_t[0])
        recv_p[...] = jnp.zeros_like(recv_p)

    spread = spread_ref[...]
    swap = swap_ref[...]

    def rotated(rows, cos_t, sin_t):
        positive = jnp.maximum(rows, jnp.zeros_like(rows))
        plain = mm(positive, spread)
        turned = mm(positive, swap)
        return plain.astype(BF16), plain * (cos_hw + cos_t) + turned * (sin_hw + sin_t)

    lane = lax.broadcasted_iota(jnp.int32, (TF, PAD), 1)
    ones = jnp.where(lane >= HD, 1.0, 0.0).astype(BF16)
    frames = []
    for t in range(FC):
        rows = slice(t * TF, (t + 1) * TF)
        k_pos, k_rot = rotated(k_ref[rows, :], time_own[t : t + 1, :], time_own[8 + t : 9 + t, :])
        k_hi, k_lo = split(k_rot)
        value = mm(v_ref[rows, :], spread).astype(BF16)
        per_head = []
        for g in range(heads):
            cut = slice(g * PAD, (g + 1) * PAD)
            per_head.append(
                mm_t(k_hi[:, cut], value[:, cut]) + mm_t(k_lo[:, cut], value[:, cut]) + mm_t(k_pos[:, cut], ones)
            )
        frames.append(jnp.concatenate(per_head, axis=0))
    id0 = fb_ref[0].astype(F32)
    id1 = fb_ref[1].astype(F32)
    own_t = frames[0] + frames[1]
    own_l = frames[0] + jnp.where(id0 == id1, 1.0, 0.0) * frames[1]
    row = lax.broadcasted_iota(jnp.int32, own_t.shape, 0)
    msg_t[...] = own_t.astype(BF16)
    msg_l[...] = jnp.where(row == HD, id0, jnp.where(row == HD + 1, id1, own_l)).astype(BF16)

    t_copies = {}
    l_copies = {}
    for k in range(1, F):
        t_copies[k] = remote(
            msg_t, recv_t.at[k - 1], t_send.at[k - 1], t_recv.at[k - 1], lax.rem(f + k, F), h
        )
    for k in range(1, reach + 1):
        l_copies[k] = remote(
            msg_l, recv_l.at[k - 1], l_send.at[k - 1], l_recv.at[k - 1], lax.rem(f - k + F, F), h
        )
    p_copy = remote(msg_l, recv_p, p_send, p_recv, nxt, h)
    for k in range(F - 1, 0, -1):

        @pl.when(f + k < F)
        def _(k=k):
            t_copies[k].start()

    @pl.when(f < F - 1)
    def _():
        p_copy.start()

    for k in range(reach, 0, -1):

        @pl.when(f >= k)
        def _(k=k):
            l_copies[k].start()

    q_parts = [None, None]
    for t in range(FC):
        rows = slice(t * TF, (t + 1) * TF)
        q_parts.append(rotated(q_ref[rows, :], time_own[t : t + 1, :], time_own[8 + t : 9 + t, :]))

    @pl.when(f > 0)
    def _():
        q_copy.wait_recv()
        t_copy.wait_recv()

    for t in range(FC):
        rows = slice(t * TF, (t + 1) * TF)
        q_parts[t] = rotated(qh[rows, :], time_prev[t : t + 1, :], time_prev[8 + t : 9 + t, :])

    state[2] = own_l
    state[3] = own_t

    @pl.when(f > 0)
    def _():
        p_copy.wait_recv()
        t_copies[1].wait_recv()

    lead_prev = recv_p[...].astype(F32)
    state[0] = lead_prev
    all_prev = recv_t[0].astype(F32)
    state[1] = all_prev
    state[2] += all_prev
    state[3] += all_prev
    ids = [lead_prev[HD : HD + 1], lead_prev[HD + 1 : HD + 2], id0, id1]

    def add_tail(i, other, lead):
        state[i] += jnp.where(other == ids[i], 1.0, 0.0) * lead

    for i in range(2):
        add_tail(i, id0, own_l)
    for k in range(1, reach + 1):

        @pl.when(f + k < F)
        def _(k=k):
            l_copies[k].wait_recv()
            lead = recv_l[k - 1].astype(F32)
            for i in range(4):
                add_tail(i, lead[HD : HD + 1], lead)

    for k in range(2, F):

        @pl.when(f >= k)
        def _(k=k):
            t_copies[k].wait_recv()
            piece = recv_t[k - 1].astype(F32)
            for i in range(4):
                state[i] += piece

    for t in range(2 + FC):
        q_pos, q_rot = q_parts[t]
        q_hi, q_lo = split(q_rot)
        full = state[t]
        merged = []
        for g in range(heads):
            cut = slice(g * PAD, (g + 1) * PAD)
            block = full[cut, :]
            s_hi, s_lo = split(block)
            total_hi, total_lo = split(jnp.broadcast_to(block[:, HD : HD + 1], (PAD, PAD)))
            numerator = mm(q_hi[:, cut], s_hi) + mm(q_lo[:, cut], s_hi) + mm(q_hi[:, cut], s_lo)
            denominator = mm(q_pos[:, cut], total_hi) + mm(q_pos[:, cut], total_lo) + EPSILON
            merged.append((numerator / denominator).astype(BF16))
        tight = mm(jnp.concatenate(merged, axis=1), gather_ref[...]).astype(BF16)
        for g in range(H):
            att[g, t] = tight[g * TD : (g + 1) * TD]

    x_copies = []
    for j in range(Y):
        x_copies.append(remote(att.at[2 * j + 1 - c], att_x.at[j], x_send.at[j], x_recv.at[j], f, mate))
        x_copies[-1].start()
    w_local.wait()
    w_far.wait_recv()
    for copy in x_copies:
        copy.wait_recv()

    starts = np.cumsum([0] + list(chunks))

    def conv(j, n):
        cols = slice(int(starts[n]), int(starts[n + 1]))
        total = None
        for tap in range(3):
            for side in range(2):
                source = att.at[2 * j + c] if side == 0 else att_x.at[j]
                rows = source[2 - tap : 2 - tap + FC].reshape(FC * TD, heads * HD)
                term = mm(rows, w_buf[side, tap, :, cols])
                total = term if total is None else total + term
        return total

    c_copies = []
    for j in range(1, Y):
        target = lax.rem(y + j, Y)
        for n in range(n_chunk):
            part_send[n][j - 1] = conv(target, n).astype(BF16)
            slot = (j - 1) * n_chunk + n
            copy = remote(
                part_send[n].at[j - 1], part_recv[n].at[j - 1], c_send.at[slot], c_recv.at[slot], f, 2 * target + c
            )
            copy.start()
            c_copies.append(copy)
    for n in range(n_chunk):
        part_own[n][...] = conv(y, n)
    for n in range(n_chunk):
        cols = slice(int(starts[n]), int(starts[n + 1]))
        total = part_own[n][...]
        for j in range(1, Y):
            c_copies[(j - 1) * n_chunk + n].wait_recv()
            total = total + part_recv[n][j - 1].astype(F32)
        total = total + bias_ref[:, cols]
        result = (total / (1.0 + jnp.exp(-total))).astype(BF16)
        for t in range(FC):
            for r in range(RD):
                start = t * TD + r * W
                out_ref[r, t, :, cols] = result[start : start + W]

    w_far.wait_send()
    for copy in x_copies + c_copies:
        copy.wait_send()

    @pl.when(f < F - 1)
    def _():
        q_copy.wait_send()
        t_copy.wait_send()
        p_copy.wait_send()

    for k in range(1, F):

        @pl.when(f + k < F)
        def _(k=k):
            t_copies[k].wait_send()

    for k in range(1, reach + 1):

        @pl.when(f >= k)
        def _(k=k):
            l_copies[k].wait_send()


def per_device(F, H, queries, key_vectors, value_vectors, frame_index, height_index, width_index, frame_block,
               conv_weight, conv_bias):
    FC, HG, W, C = queries.shape
    heads = C // HD
    assert FC == 2 and H % 2 == 0
    Y = H // 2
    T, TF, RD = FC * HG * W, HG * W, HG // H
    TD = RD * W
    O = conv_weight.shape[-1]
    chunks = [COLUMNS] * (O // COLUMNS) + ([O % COLUMNS] if O % COLUMNS else [])
    spread, swap, freq = tables(heads)
    positions = jnp.concatenate(
        [width_index, height_index, frame_index, jnp.zeros((8 - FC,), jnp.int32)]
    ).astype(F32)[:, None]
    reach = min(F - 1, -(-(BLOCK_MOST - 1) // FC))
    lanes = heads * PAD
    vmem = pl.BlockSpec(memory_space=pltpu.VMEM)
    dma = pltpu.SemaphoreType.DMA
    return pl.pallas_call(
        functools.partial(kernel, (F, Y, heads, HG, W, tuple(chunks))),
        out_shape=jax.ShapeDtypeStruct((RD, FC, W, O), BF16),
        in_specs=[pl.BlockSpec(memory_space=pltpu.SMEM)] + [vmem] * 8 + [pl.BlockSpec(memory_space=pl.ANY), vmem],
        out_specs=vmem,
        scratch_shapes=[
            pltpu.VMEM((2,) + conv_weight.shape, BF16),
            pltpu.VMEM((T, C), BF16),
            pltpu.VMEM((16, lanes), F32),
            pltpu.VMEM((16, lanes), F32),
            pltpu.VMEM((lanes, PAD), BF16),
            pltpu.VMEM((lanes, PAD), BF16),
            pltpu.VMEM((max(F - 1, 1), lanes, PAD), BF16),
            pltpu.VMEM((max(reach, 1), lanes, PAD), BF16),
            pltpu.VMEM((lanes, PAD), BF16),
            pltpu.VMEM((4, lanes, PAD), F32),
            pltpu.VMEM((H, 2 + FC, TD, C), BF16),
            pltpu.VMEM((Y, 2 + FC, TD, C), BF16),
        ]
        + [pltpu.VMEM((max(Y - 1, 1), FC * TD, n), BF16) for n in chunks]
        + [pltpu.VMEM((max(Y - 1, 1), FC * TD, n), BF16) for n in chunks]
        + [pltpu.VMEM((FC * TD, n), F32) for n in chunks]
        + [
            dma, dma, dma, dma((2,)), dma((2,)),
            dma((max(F - 1, 1),)), dma((max(F - 1, 1),)),
            dma((max(reach, 1),)), dma((max(reach, 1),)),
            dma, dma,
            dma((Y,)), dma((Y,)),
            dma((max(Y - 1, 1) * len(chunks),)), dma((max(Y - 1, 1) * len(chunks),)),
        ],
        compiler_params=pltpu.CompilerParams(
            collective_id=0, has_side_effects=True, vmem_limit_bytes=48 * 1024 * 1024
        ),
        name="attend_conv",
    )(
        frame_block,
        queries.reshape(T, C),
        key_vectors.reshape(T, C),
        value_vectors.reshape(T, C),
        positions,
        jnp.asarray(freq),
        jnp.asarray(spread, BF16),
        jnp.asarray(swap, BF16),
        jnp.asarray(spread.T, BF16),
        conv_weight,
        conv_bias[None, :],
    )


def solution(mesh):
    placed = (
        P("frame", None, None, "head"),
        P("frame", None, None, "head"),
        P("frame", None, None, "head"),
        P("frame"),
        P(),
        P(),
        P("frame"),
        P(None, "head", None),
        P(),
    )
    return jax.shard_map(
        functools.partial(per_device, mesh.shape["frame"], mesh.shape["head"]),
        mesh=mesh,
        in_specs=placed,
        out_specs=P("head", "frame", None, None),
        check_vma=False,
    )
```

```python
import functools

import jax
import jax.numpy as jnp
import numpy as np
from jax import lax
from jax.experimental import pallas as pl
from jax.experimental.pallas import tpu as pltpu
from jax.sharding import PartitionSpec as P

HD = 112
PAD = 128
EPSILON = 1e-06
BLOCK_MOST = 6
COLUMNS = 512
F32 = jnp.float32
BF16 = jnp.bfloat16


def sections():
    side = HD * 5 // 14 // 2 * 2
    first = HD - 2 * side
    return ((0, first), (first, side), (first + side, side))


def tables(heads):
    C, lanes = heads * HD, heads * PAD
    lane = lax.broadcasted_iota(jnp.int32, (1, lanes), 1)
    head, d = lane // PAD, lane % PAD
    inside = d < HD
    source = jnp.where(inside, head * HD + d, -1)
    partner, sign = jnp.full_like(lane, -1), jnp.zeros((1, lanes), F32)
    freqs, masks = [], []
    for start, n in sections():
        half = n // 2
        low = (d >= start) & (d < start + half)
        high = (d >= start + half) & (d < start + n)
        partner = jnp.where(low, source + half, jnp.where(high, source - half, partner))
        sign = jnp.where(low, -1.0, jnp.where(high, 1.0, sign))
        j = jnp.where(low, d - start, d - start - half).astype(F32)
        either = low | high
        freqs.append(jnp.where(either, jnp.exp(j * float(-2.0 * np.log(10000.0) / n)), 0.0))
        masks.append(jnp.where(either, 1.0, 0.0))
    row = lax.broadcasted_iota(jnp.int32, (C, lanes), 0)
    spread = jnp.where(row == source, 1.0, 0.0).astype(BF16)
    swap = jnp.where(row == partner, sign, 0.0).astype(BF16)
    column = lax.broadcasted_iota(jnp.int32, (1, C), 1)
    target = column // HD * PAD + column % HD
    row = lax.broadcasted_iota(jnp.int32, (lanes, C), 0)
    gather = jnp.where(row == target, 1.0, 0.0).astype(BF16)
    return spread, swap, gather, freqs, masks


def positions(ref, count, rows, lanes):
    row = lax.broadcasted_iota(jnp.int32, (rows, lanes), 0)
    result = jnp.zeros((rows, lanes), F32)
    for i in range(count):
        result = jnp.where(row == i, ref[i].astype(F32), result)
    return result


def mm(a, b):
    return jnp.dot(a, b, preferred_element_type=F32)


def mm_t(a, b):
    return lax.dot_general(a, b, (((0,), (0,)), ((), ())), preferred_element_type=F32)


def split(a):
    high = a.astype(BF16)
    return high, (a - high.astype(F32)).astype(BF16)


def kernel(
    cfg, q_any, k_any, v_any, fi_any, hi_any, wi_any, fb_any, w_ref, bias_any, out_ref,
    q_ref, k_ref, v_ref, fi_ref, hi_ref, wi_ref, fb_ref, bias_ref, in_sem, w_buf, qh, time_own, time_prev, msg_t, msg_l, recv_t, recv_l, recv_p, state, att, att_x, *rest,
):
    F, Y, heads, HG, W, chunks = cfg
    n_chunk = len(chunks)
    part_send, part_recv, part_own = rest[:n_chunk], rest[n_chunk : 2 * n_chunk], rest[2 * n_chunk : 3 * n_chunk]
    (w_sem, w_send, w_recv, halo_send, halo_recv, t_send, t_recv, l_send, l_recv, p_send, p_recv,
     x_send, x_recv, c_send, c_recv) = rest[3 * n_chunk :]
    FC = 2
    H = 2 * Y
    TF = HG * W
    RD = HG // H
    TD = RD * W
    reach = min(F - 1, -(-(BLOCK_MOST - 1) // FC))
    f = lax.axis_index("frame")
    h = lax.axis_index("head")
    y, c = h // 2, h % 2
    mate = 2 * y + (1 - c)

    loads = [
        pltpu.make_async_copy(src, dst, in_sem.at[i])
        for i, (src, dst) in enumerate(
            [(fi_any, fi_ref), (hi_any, hi_ref), (wi_any, wi_ref), (fb_any, fb_ref), (k_any, k_ref), (v_any, v_ref),
             (q_any, q_ref), (bias_any, bias_ref)]
        )
    ]
    for load in loads:
        load.start()

    barrier = pltpu.get_barrier_semaphore()
    for k in range(1, F):
        pl.semaphore_signal(barrier, inc=1, device_id=(lax.rem(f + k, F), h), device_id_type=pl.DeviceIdType.MESH)
    pl.semaphore_signal(barrier, inc=1, device_id=(f, mate), device_id_type=pl.DeviceIdType.MESH)
    for j in range(1, Y):
        pl.semaphore_signal(
            barrier, inc=1, device_id=(f, 2 * lax.rem(y + j, Y) + c), device_id_type=pl.DeviceIdType.MESH
        )

    def remote(src, dst, send, recv, frame, head):
        return pltpu.make_async_remote_copy(
            src_ref=src, dst_ref=dst, send_sem=send, recv_sem=recv,
            device_id=(frame, head), device_id_type=pl.DeviceIdType.MESH,
        )

    w_local = pltpu.make_async_copy(w_ref, w_buf.at[0], w_sem)
    w_local.start()

    lanes = heads * PAD
    spread, swap, gather, freqs, masks = tables(heads)
    for load in loads[:4]:
        load.wait()
    t_ang = positions(fi_ref, FC, 8, lanes) * freqs[0]
    time_own[0:8, :] = jnp.cos(t_ang) * masks[0]
    time_own[8:16, :] = jnp.sin(t_ang)
    h_ang = positions(hi_ref, HG, HG, lanes) * freqs[1]
    w_ang = positions(wi_ref, W, W, lanes) * freqs[2]
    cos_hw = (
        (jnp.cos(h_ang) * masks[1]).reshape(HG, 1, lanes) + (jnp.cos(w_ang) * masks[2]).reshape(1, W, lanes)
    ).reshape(TF, lanes)
    sin_hw = (jnp.sin(h_ang).reshape(HG, 1, lanes) + jnp.sin(w_ang).reshape(1, W, lanes)).reshape(TF, lanes)

    pl.semaphore_wait(barrier, (F - 1) + 1 + (Y - 1))

    w_far = remote(w_ref, w_buf.at[1], w_send, w_recv, f, mate)
    w_far.start()
    nxt = lax.rem(f + 1, F)
    q_copy = remote(q_any, qh, halo_send.at[0], halo_recv.at[0], nxt, h)
    t_copy = remote(time_own, time_prev, halo_send.at[1], halo_recv.at[1], nxt, h)

    @pl.when(f < F - 1)
    def _():
        q_copy.start()
        t_copy.start()

    @pl.when(f == 0)
    def _():
        qh[...] = jnp.zeros_like(qh)
        time_prev[...] = jnp.zeros_like(time_prev)
        recv_t[0] = jnp.zeros_like(recv_t[0])
        recv_p[...] = jnp.zeros_like(recv_p)


    def rotated(rows, cos_t, sin_t):
        positive = jnp.maximum(rows, jnp.zeros_like(rows))
        plain = mm(positive, spread)
        turned = mm(positive, swap)
        return plain.astype(BF16), plain * (cos_hw + cos_t) + turned * (sin_hw + sin_t)

    lane = lax.broadcasted_iota(jnp.int32, (TF, PAD), 1)
    ones = jnp.where(lane >= HD, 1.0, 0.0).astype(BF16)
    for load in loads[4:6]:
        load.wait()
    frames = []
    for t in range(FC):
        rows = slice(t * TF, (t + 1) * TF)
        k_pos, k_rot = rotated(k_ref[rows, :], time_own[t : t + 1, :], time_own[8 + t : 9 + t, :])
        k_hi, k_lo = split(k_rot)
        value = mm(v_ref[rows, :], spread).astype(BF16)
        per_head = []
        for g in range(heads):
            cut = slice(g * PAD, (g + 1) * PAD)
            per_head.append(
                mm_t(k_hi[:, cut], value[:, cut]) + mm_t(k_lo[:, cut], value[:, cut]) + mm_t(k_pos[:, cut], ones)
            )
        frames.append(jnp.concatenate(per_head, axis=0))
    id0 = fb_ref[0].astype(F32)
    id1 = fb_ref[1].astype(F32)
    own_t = frames[0] + frames[1]
    own_l = frames[0] + jnp.where(id0 == id1, 1.0, 0.0) * frames[1]
    row = lax.broadcasted_iota(jnp.int32, own_t.shape, 0)
    msg_t[...] = own_t.astype(BF16)
    msg_l[...] = jnp.where(row == HD, id0, jnp.where(row == HD + 1, id1, own_l)).astype(BF16)

    t_copies = {}
    l_copies = {}
    for k in range(1, F):
        t_copies[k] = remote(
            msg_t, recv_t.at[k - 1], t_send.at[k - 1], t_recv.at[k - 1], lax.rem(f + k, F), h
        )
    for k in range(1, reach + 1):
        l_copies[k] = remote(
            msg_l, recv_l.at[k - 1], l_send.at[k - 1], l_recv.at[k - 1], lax.rem(f - k + F, F), h
        )
    p_copy = remote(msg_l, recv_p, p_send, p_recv, nxt, h)
    for k in range(F - 1, 0, -1):

        @pl.when(f + k < F)
        def _(k=k):
            t_copies[k].start()

    @pl.when(f < F - 1)
    def _():
        p_copy.start()

    for k in range(reach, 0, -1):

        @pl.when(f >= k)
        def _(k=k):
            l_copies[k].start()

    loads[6].wait()
    q_parts = [None, None]
    for t in range(FC):
        rows = slice(t * TF, (t + 1) * TF)
        q_parts.append(rotated(q_ref[rows, :], time_own[t : t + 1, :], time_own[8 + t : 9 + t, :]))

    @pl.when(f > 0)
    def _():
        q_copy.wait_recv()
        t_copy.wait_recv()

    for t in range(FC):
        rows = slice(t * TF, (t + 1) * TF)
        q_parts[t] = rotated(qh[rows, :], time_prev[t : t + 1, :], time_prev[8 + t : 9 + t, :])

    state[2] = own_l
    state[3] = own_t

    @pl.when(f > 0)
    def _():
        p_copy.wait_recv()
        t_copies[1].wait_recv()

    lead_prev = recv_p[...].astype(F32)
    state[0] = lead_prev
    all_prev = recv_t[0].astype(F32)
    state[1] = all_prev
    state[2] += all_prev
    state[3] += all_prev
    ids = [lead_prev[HD : HD + 1], lead_prev[HD + 1 : HD + 2], id0, id1]

    def add_tail(i, other, lead):
        state[i] += jnp.where(other == ids[i], 1.0, 0.0) * lead

    for i in range(2):
        add_tail(i, id0, own_l)
    for k in range(1, reach + 1):

        @pl.when(f + k < F)
        def _(k=k):
            l_copies[k].wait_recv()
            lead = recv_l[k - 1].astype(F32)
            for i in range(4):
                add_tail(i, lead[HD : HD + 1], lead)

    for k in range(2, F):

        @pl.when(f >= k)
        def _(k=k):
            t_copies[k].wait_recv()
            piece = recv_t[k - 1].astype(F32)
            for i in range(4):
                state[i] += piece

    for t in range(2 + FC):
        q_pos, q_rot = q_parts[t]
        q_hi, q_lo = split(q_rot)
        full = state[t]
        merged = []
        for g in range(heads):
            cut = slice(g * PAD, (g + 1) * PAD)
            block = full[cut, :]
            s_hi, s_lo = split(block)
            total_hi, total_lo = split(jnp.broadcast_to(block[:, HD : HD + 1], (PAD, PAD)))
            numerator = mm(q_hi[:, cut], s_hi) + mm(q_lo[:, cut], s_hi) + mm(q_hi[:, cut], s_lo)
            denominator = mm(q_pos[:, cut], total_hi) + mm(q_pos[:, cut], total_lo) + EPSILON
            merged.append((numerator / denominator).astype(BF16))
        tight = mm(jnp.concatenate(merged, axis=1), gather).astype(BF16)
        for g in range(H):
            att[g, t] = tight[g * TD : (g + 1) * TD]

    x_copies = []
    for j in range(Y):
        x_copies.append(remote(att.at[2 * j + 1 - c], att_x.at[j], x_send.at[j], x_recv.at[j], f, mate))
        x_copies[-1].start()
    w_local.wait()
    w_far.wait_recv()
    for copy in x_copies:
        copy.wait_recv()

    starts = np.cumsum([0] + list(chunks))

    def conv(j, n):
        cols = slice(int(starts[n]), int(starts[n + 1]))
        total = None
        for tap in range(3):
            for side in range(2):
                source = att.at[2 * j + c] if side == 0 else att_x.at[j]
                rows = source[2 - tap : 2 - tap + FC].reshape(FC * TD, heads * HD)
                term = mm(rows, w_buf[side, tap, :, cols])
                total = term if total is None else total + term
        return total

    c_copies = []
    for j in range(1, Y):
        target = lax.rem(y + j, Y)
        for n in range(n_chunk):
            part_send[n][j - 1] = conv(target, n).astype(BF16)
            slot = (j - 1) * n_chunk + n
            copy = remote(
                part_send[n].at[j - 1], part_recv[n].at[j - 1], c_send.at[slot], c_recv.at[slot], f, 2 * target + c
            )
            copy.start()
            c_copies.append(copy)
    for n in range(n_chunk):
        part_own[n][...] = conv(y, n)
    loads[7].wait()
    bias = bias_ref[...].reshape(1, -1)
    for n in range(n_chunk):
        cols = slice(int(starts[n]), int(starts[n + 1]))
        total = part_own[n][...]
        for j in range(1, Y):
            c_copies[(j - 1) * n_chunk + n].wait_recv()
            total = total + part_recv[n][j - 1].astype(F32)
        total = total + bias[:, cols]
        result = (total / (1.0 + jnp.exp(-total))).astype(BF16)
        for t in range(FC):
            for r in range(RD):
                start = t * TD + r * W
                out_ref[r, t, :, cols] = result[start : start + W]

    w_far.wait_send()
    for copy in x_copies + c_copies:
        copy.wait_send()

    @pl.when(f < F - 1)
    def _():
        q_copy.wait_send()
        t_copy.wait_send()
        p_copy.wait_send()

    for k in range(1, F):

        @pl.when(f + k < F)
        def _(k=k):
            t_copies[k].wait_send()

    for k in range(1, reach + 1):

        @pl.when(f >= k)
        def _(k=k):
            l_copies[k].wait_send()


def per_device(F, H, queries, key_vectors, value_vectors, frame_index, height_index, width_index, frame_block,
               conv_weight, conv_bias):
    FC, HG, W, C = queries.shape
    heads = C // HD
    assert FC == 2 and H % 2 == 0
    Y = H // 2
    T, TF, RD = FC * HG * W, HG * W, HG // H
    TD = RD * W
    O = conv_weight.shape[-1]
    chunks = [COLUMNS] * (O // COLUMNS) + ([O % COLUMNS] if O % COLUMNS else [])
    reach = min(F - 1, -(-(BLOCK_MOST - 1) // FC))
    lanes = heads * PAD
    vmem = pl.BlockSpec(memory_space=pltpu.VMEM)
    dma = pltpu.SemaphoreType.DMA
    return pl.pallas_call(
        functools.partial(kernel, (F, Y, heads, HG, W, tuple(chunks))),
        out_shape=jax.ShapeDtypeStruct((RD, FC, W, O), BF16),
        in_specs=[pl.BlockSpec(memory_space=pl.ANY)] * 9,
        out_specs=vmem,
        scratch_shapes=[
            pltpu.VMEM((T, C), BF16),
            pltpu.VMEM((T, C), BF16),
            pltpu.VMEM((T, C), BF16),
            pltpu.SMEM((FC,), jnp.int32),
            pltpu.SMEM((HG,), jnp.int32),
            pltpu.SMEM((W,), jnp.int32),
            pltpu.SMEM((FC,), jnp.int32),
            pltpu.VMEM((O,), F32),
            dma((8,)),
            pltpu.VMEM((2,) + conv_weight.shape, BF16),
            pltpu.VMEM((T, C), BF16),
            pltpu.VMEM((16, lanes), F32),
            pltpu.VMEM((16, lanes), F32),
            pltpu.VMEM((lanes, PAD), BF16),
            pltpu.VMEM((lanes, PAD), BF16),
            pltpu.VMEM((max(F - 1, 1), lanes, PAD), BF16),
            pltpu.VMEM((max(reach, 1), lanes, PAD), BF16),
            pltpu.VMEM((lanes, PAD), BF16),
            pltpu.VMEM((4, lanes, PAD), F32),
            pltpu.VMEM((H, 2 + FC, TD, C), BF16),
            pltpu.VMEM((Y, 2 + FC, TD, C), BF16),
        ]
        + [pltpu.VMEM((max(Y - 1, 1), FC * TD, n), BF16) for n in chunks]
        + [pltpu.VMEM((max(Y - 1, 1), FC * TD, n), BF16) for n in chunks]
        + [pltpu.VMEM((FC * TD, n), F32) for n in chunks]
        + [
            dma, dma, dma, dma((2,)), dma((2,)),
            dma((max(F - 1, 1),)), dma((max(F - 1, 1),)),
            dma((max(reach, 1),)), dma((max(reach, 1),)),
            dma, dma,
            dma((Y,)), dma((Y,)),
            dma((max(Y - 1, 1) * len(chunks),)), dma((max(Y - 1, 1) * len(chunks),)),
        ],
        compiler_params=pltpu.CompilerParams(
            collective_id=0, has_side_effects=True, vmem_limit_bytes=60 * 1024 * 1024
        ),
        name="attend_conv",
    )(
        queries.reshape(T, C),
        key_vectors.reshape(T, C),
        value_vectors.reshape(T, C),
        frame_index,
        height_index,
        width_index,
        frame_block,
        conv_weight,
        conv_bias,
    )


def solution(mesh):
    placed = (
        P("frame", None, None, "head"),
        P("frame", None, None, "head"),
        P("frame", None, None, "head"),
        P("frame"),
        P(),
        P(),
        P("frame"),
        P(None, "head", None),
        P(),
    )
    return jax.shard_map(
        functools.partial(per_device, mesh.shape["frame"], mesh.shape["head"]),
        mesh=mesh,
        in_specs=placed,
        out_specs=P("head", "frame", None, None),
        check_vma=False,
    )
```

```python
import functools

import jax
import jax.numpy as jnp
import numpy as np
from jax import lax
from jax.experimental import pallas as pl
from jax.experimental.pallas import tpu as pltpu
from jax.sharding import PartitionSpec as P

HD = 112
PAD = 128
EPSILON = 1e-06
BLOCK_MOST = 6
COLUMNS = 512
F32 = jnp.float32
BF16 = jnp.bfloat16


def sections():
    side = HD * 5 // 14 // 2 * 2
    first = HD - 2 * side
    return ((0, first), (first, side), (first + side, side))


def tables(heads):
    C, lanes = heads * HD, heads * PAD
    lane = lax.broadcasted_iota(jnp.int32, (1, lanes), 1)
    head, d = lane // PAD, lane % PAD
    inside = d < HD
    source = jnp.where(inside, head * HD + d, -1)
    partner, sign = jnp.full_like(lane, -1), jnp.zeros((1, lanes), F32)
    freqs, masks = [], []
    for start, n in sections():
        half = n // 2
        low = (d >= start) & (d < start + half)
        high = (d >= start + half) & (d < start + n)
        partner = jnp.where(low, source + half, jnp.where(high, source - half, partner))
        sign = jnp.where(low, -1.0, jnp.where(high, 1.0, sign))
        j = jnp.where(low, d - start, d - start - half).astype(F32)
        either = low | high
        freqs.append(jnp.where(either, jnp.exp(j * float(-2.0 * np.log(10000.0) / n)), 0.0))
        masks.append(jnp.where(either, 1.0, 0.0))
    row = lax.broadcasted_iota(jnp.int32, (C, lanes), 0)
    spread = jnp.where(row == source, 1.0, 0.0).astype(BF16)
    swap = jnp.where(row == partner, sign, 0.0).astype(BF16)
    column = lax.broadcasted_iota(jnp.int32, (1, C), 1)
    target = column // HD * PAD + column % HD
    row = lax.broadcasted_iota(jnp.int32, (lanes, C), 0)
    gather = jnp.where(row == target, 1.0, 0.0).astype(BF16)
    return spread, swap, gather, freqs, masks


def positions(ref, count, rows, lanes):
    row = lax.broadcasted_iota(jnp.int32, (rows, lanes), 0)
    result = jnp.zeros((rows, lanes), F32)
    for i in range(count):
        result = jnp.where(row == i, ref[i].astype(F32), result)
    return result


def mm(a, b):
    return jnp.dot(a, b, preferred_element_type=F32)


def mm_t(a, b):
    return lax.dot_general(a, b, (((0,), (0,)), ((), ())), preferred_element_type=F32)


def mm_n(a, b):
    return lax.dot_general(a, b, (((1,), (1,)), ((), ())), preferred_element_type=F32)


def split(a):
    high = a.astype(BF16)
    return high, (a - high.astype(F32)).astype(BF16)


def kernel(
    cfg, q_any, k_any, v_any, fi_any, hi_any, wi_any, fb_any, w_ref, bias_any, out_ref,
    q_ref, k_ref, v_ref, fi_ref, hi_ref, wi_ref, fb_ref, bias_ref, in_sem, w_buf, qh, time_own, time_prev, msg_t, msg_l, msg_n, msg_r, msg_j, recv_t, recv_l, recv_n, recv_r, recv_j, base, state, att, att_x, *rest,
):
    F, Y, heads, HG, W, chunks = cfg
    n_chunk = len(chunks)
    part_send, part_recv, part_own = rest[:n_chunk], rest[n_chunk : 2 * n_chunk], rest[2 * n_chunk : 3 * n_chunk]
    (w_sem, w_send, w_recv, halo_send, halo_recv, t_send, t_recv, l_send, l_recv, p_send, p_recv,
          x_send, x_recv, c_send, c_recv) = rest[3 * n_chunk :]
    FC = 2
    H = 2 * Y
    TF = HG * W
    RD = HG // H
    TD = RD * W
    O = F // 2
    reach = -(-(BLOCK_MOST - 1) // FC)
    down = (reach + 1) // 2
    f = lax.axis_index("frame")
    h = lax.axis_index("head")
    y, c = h // 2, h % 2
    mate = 2 * y + (1 - c)
    inner, outer = f % 2, f // 2
    partner = f + 1 - 2 * inner

    loads = [
        pltpu.make_async_copy(src, dst, in_sem.at[i])
        for i, (src, dst) in enumerate(
            [(fi_any, fi_ref), (hi_any, hi_ref), (wi_any, wi_ref), (fb_any, fb_ref), (k_any, k_ref), (v_any, v_ref),
             (q_any, q_ref), (bias_any, bias_ref)]
        )
    ]
    for load in loads:
        load.start()

    barrier = pltpu.get_barrier_semaphore()
    for k in range(1, F):
        pl.semaphore_signal(barrier, inc=1, device_id=(lax.rem(f + k, F), h), device_id_type=pl.DeviceIdType.MESH)
    pl.semaphore_signal(barrier, inc=1, device_id=(f, mate), device_id_type=pl.DeviceIdType.MESH)
    for j in range(1, Y):
        pl.semaphore_signal(
            barrier, inc=1, device_id=(f, 2 * lax.rem(y + j, Y) + c), device_id_type=pl.DeviceIdType.MESH
        )

    def remote(src, dst, send, recv, frame, head):
        return pltpu.make_async_remote_copy(
            src_ref=src, dst_ref=dst, send_sem=send, recv_sem=recv,
            device_id=(frame, head), device_id_type=pl.DeviceIdType.MESH,
        )

    w_local = pltpu.make_async_copy(w_ref, w_buf.at[0], w_sem)
    w_local.start()

    lanes = heads * PAD
    spread, swap, gather, freqs, masks = tables(heads)
    for load in loads[:4]:
        load.wait()
    t_ang = positions(fi_ref, FC, 8, lanes) * freqs[0]
    time_own[0:8, :] = jnp.cos(t_ang) * masks[0]
    time_own[8:16, :] = jnp.sin(t_ang)
    h_ang = positions(hi_ref, HG, HG, lanes) * freqs[1]
    w_ang = positions(wi_ref, W, W, lanes) * freqs[2]
    cos_hw = (
        (jnp.cos(h_ang) * masks[1]).reshape(HG, 1, lanes) + (jnp.cos(w_ang) * masks[2]).reshape(1, W, lanes)
    ).reshape(TF, lanes)
    sin_hw = (jnp.sin(h_ang).reshape(HG, 1, lanes) + jnp.sin(w_ang).reshape(1, W, lanes)).reshape(TF, lanes)

    pl.semaphore_wait(barrier, (F - 1) + 1 + (Y - 1))

    w_far = remote(w_ref, w_buf.at[1], w_send, w_recv, f, mate)
    w_far.start()
    nxt = lax.rem(f + 1, F)
    q_copy = remote(q_any, qh, halo_send.at[0], halo_recv.at[0], nxt, h)
    t_copy = remote(time_own, time_prev, halo_send.at[1], halo_recv.at[1], nxt, h)

    @pl.when(f < F - 1)
    def _():
        q_copy.start()
        t_copy.start()

    @pl.when(f == 0)
    def _():
        qh[...] = jnp.zeros_like(qh)
        time_prev[...] = jnp.zeros_like(time_prev)
        recv_n[...] = jnp.zeros_like(recv_n)


    def rotated(rows, cos_t, sin_t):
        positive = jnp.maximum(rows, jnp.zeros_like(rows))
        plain = mm(positive, spread)
        turned = mm(positive, swap)
        return plain.astype(BF16), plain * (cos_hw + cos_t) + turned * (sin_hw + sin_t)

    ones = jnp.where(lax.broadcasted_iota(jnp.int32, (PAD, TF), 0) >= HD, 1.0, 0.0).astype(BF16)
    for load in loads[4:6]:
        load.wait()
    frames = []
    for t in range(FC):
        rows = slice(t * TF, (t + 1) * TF)
        k_pos, k_rot = rotated(k_ref[rows, :], time_own[t : t + 1, :], time_own[8 + t : 9 + t, :])
        k_hi, k_lo = split(k_rot)
        value = mm(v_ref[rows, :], spread).astype(BF16)
        per_head = []
        totals = mm(ones, k_pos)
        for g in range(heads):
            cut = slice(g * PAD, (g + 1) * PAD)
            both = mm_t(value[:, cut], jnp.concatenate([k_hi[:, cut], k_lo[:, cut]], axis=1))
            per_head.append(both[:, :PAD] + both[:, PAD:] + totals[:, cut])
        frames.append(jnp.concatenate(per_head, axis=0))
    id0 = fb_ref[0].astype(F32)
    id1 = fb_ref[1].astype(F32)
    same = jnp.where(id0 == id1, 1.0, 0.0)
    own_t = frames[0] + frames[1]
    own_l = frames[0] + same * frames[1]
    row = lax.broadcasted_iota(jnp.int32, own_t.shape, 0)

    def tagged(value, first, second):
        return jnp.where(row == HD + 1, first, jnp.where(row == HD + 2, second, value)).astype(BF16)

    msg_t[...] = own_t.astype(BF16)
    msg_l[...] = tagged(own_l, id0, id1)
    msg_n[...] = tagged((same - 1.0) * frames[1], id0, id1)

    t_copies, l_copies, l_sends, l_gets = {}, {}, {}, {}
    for k in range(1, O):
        t_copies[k] = remote(
            msg_t, recv_t.at[k - 1], t_send.at[k - 1], t_recv.at[k - 1], lax.rem(f + 2 * k, F), h
        )
    for k in range(1, down + 1):
        l_copies[k] = remote(
            msg_l, recv_l.at[k - 1], l_send.at[k - 1], l_recv.at[k - 1], lax.rem(f - 2 * k + 2 * F, F), h
        )
        wanted = 2 * k <= reach + 1 - inner
        l_sends[k] = wanted & (outer >= k)
        l_gets[k] = wanted & (outer + k < O)
    n_copy = remote(msg_n, recv_n, p_send.at[0], p_recv.at[0], nxt, h)
    r_copy = remote(msg_r, recv_r, p_send.at[1], p_recv.at[1], partner, h)
    j_copy = remote(msg_j, recv_j, p_send.at[2], p_recv.at[2], partner, h)
    for k in range(O - 1, 0, -1):

        @pl.when(outer + k < O)
        def _(k=k):
            t_copies[k].start()

    for k in range(down, 0, -1):

        @pl.when(l_sends[k])
        def _(k=k):
            l_copies[k].start()

    @pl.when(f < F - 1)
    def _():
        n_copy.start()

    loads[6].wait()
    q_parts = [None, None]
    for t in range(FC):
        rows = slice(t * TF, (t + 1) * TF)
        q_parts.append(rotated(q_ref[rows, :], time_own[t : t + 1, :], time_own[8 + t : 9 + t, :]))

    @pl.when(inner == 0)
    def _():
        base[...] = own_t

    @pl.when(inner == 1)
    def _():
        base[...] = jnp.zeros_like(own_t)

    for k in range(1, O):

        @pl.when(outer >= k)
        def _(k=k):
            t_copies[k].wait_recv()
            base[...] += recv_t[k - 1].astype(F32)

    msg_r[...] = base[...].astype(BF16)
    r_copy.start()

    for k in range(1, down + 1):

        @pl.when(l_gets[k])
        def _(k=k):
            l_copies[k].wait_recv()

        @pl.when(jnp.logical_not(l_gets[k]))
        def _(k=k):
            recv_l[k - 1] = tagged(jnp.zeros_like(own_t), -1.0, -1.0)

    def joined(ident, total, pieces):
        for piece in pieces:
            total = total + jnp.where(piece[HD + 1 : HD + 2] == ident, 1.0, 0.0) * piece
        return tagged(total, ident, ident)

    leads = [recv_l[k].astype(F32) for k in range(down)]

    @pl.when(inner == 0)
    def _():
        msg_j[...] = joined(leads[0][HD + 1 : HD + 2], leads[0], leads[1:])

    @pl.when(inner == 1)
    def _():
        msg_j[...] = joined(id0, own_l, leads[:1])

    j_copy.start()

    @pl.when(f > 0)
    def _():
        q_copy.wait_recv()
        t_copy.wait_recv()

    for t in range(FC):
        rows = slice(t * TF, (t + 1) * TF)
        q_parts[t] = rotated(qh[rows, :], time_prev[t : t + 1, :], time_prev[8 + t : 9 + t, :])

    @pl.when(f > 0)
    def _():
        n_copy.wait_recv()

    r_copy.wait_recv()
    j_copy.wait_recv()
    before = base[...] + recv_r[...].astype(F32) - jnp.where(inner == 0, 1.0, 0.0) * own_t
    less = recv_n[...].astype(F32)
    tails = [recv_j[...].astype(F32)] + leads
    ids = [less[HD + 1 : HD + 2], less[HD + 2 : HD + 3], id0, id1]
    starts = [before + less, before, before + own_l, before + own_t]
    for i in range(2 + FC):
        total = starts[i]
        if i < 2:
            total = total + jnp.where(ids[i] == id0, 1.0, 0.0) * own_l
        for tail in tails:
            total = total + jnp.where(tail[HD + 1 : HD + 2] == ids[i], 1.0, 0.0) * tail
        state[i] = total

    for t in range(2 + FC):
        q_pos, q_rot = q_parts[t]
        q_hi, q_lo = split(q_rot)
        full = state[t]
        merged = []
        for g in range(heads):
            cut = slice(g * PAD, (g + 1) * PAD)
            block = full[cut, :]
            s_hi, s_lo = split(block)
            total_hi, total_lo = split(jnp.broadcast_to(block[HD : HD + 1, :], (PAD, PAD)))
            both = mm_n(q_hi[:, cut], jnp.concatenate([s_hi, s_lo], axis=0))
            numerator = both[:, :PAD] + both[:, PAD:] + mm_n(q_lo[:, cut], s_hi)
            both = mm_n(q_pos[:, cut], jnp.concatenate([total_hi, total_lo], axis=0))
            denominator = both[:, :PAD] + both[:, PAD:] + EPSILON
            merged.append((numerator / denominator).astype(BF16))
        tight = mm(jnp.concatenate(merged, axis=1), gather).astype(BF16)
        for g in range(H):
            att[g, t] = tight[g * TD : (g + 1) * TD]

    x_copies = []
    for j in range(Y):
        x_copies.append(remote(att.at[2 * j + 1 - c], att_x.at[j], x_send.at[j], x_recv.at[j], f, mate))
        x_copies[-1].start()
    w_local.wait()
    w_far.wait_recv()
    for copy in x_copies:
        copy.wait_recv()

    starts = np.cumsum([0] + list(chunks))
    owners = [lax.rem(y + j, Y) for j in range(1, Y)] + [y]
    M = FC * TD
    taps = []
    for tap in range(3):
        for side in range(2):
            rows = [(att.at[2 * j + c] if side == 0 else att_x.at[j])[2 - tap : 2 - tap + FC] for j in owners]
            taps.append((tap, side, jnp.concatenate([r.reshape(M, heads * HD) for r in rows], axis=0)))

    c_copies = {}
    for n in range(n_chunk):
        cols = slice(int(starts[n]), int(starts[n + 1]))
        total = None
        for tap, side, rows in taps:
            term = mm(rows, w_buf[side, tap, :, cols])
            total = term if total is None else total + term
        for j in range(1, Y):
            part_send[n][j - 1] = total[(j - 1) * M : j * M].astype(BF16)
            slot = (j - 1) * n_chunk + n
            c_copies[j, n] = remote(
                part_send[n].at[j - 1], part_recv[n].at[j - 1], c_send.at[slot], c_recv.at[slot], f,
                2 * owners[j - 1] + c,
            )
            c_copies[j, n].start()
        part_own[n][...] = total[(Y - 1) * M :]
    loads[7].wait()
    bias = bias_ref[...].reshape(1, -1)
    for n in range(n_chunk):
        cols = slice(int(starts[n]), int(starts[n + 1]))
        total = part_own[n][...]
        for j in range(1, Y):
            c_copies[j, n].wait_recv()
            total = total + part_recv[n][j - 1].astype(F32)
        total = total + bias[:, cols]
        result = (total / (1.0 + jnp.exp(-total))).astype(BF16)
        for t in range(FC):
            for r in range(RD):
                start = t * TD + r * W
                out_ref[r, t, :, cols] = result[start : start + W]

    w_far.wait_send()
    for copy in x_copies + list(c_copies.values()):
        copy.wait_send()

    @pl.when(f < F - 1)
    def _():
        q_copy.wait_send()
        t_copy.wait_send()
        n_copy.wait_send()

    r_copy.wait_send()
    j_copy.wait_send()
    for k in range(1, O):

        @pl.when(outer + k < O)
        def _(k=k):
            t_copies[k].wait_send()

    for k in range(1, down + 1):

        @pl.when(l_sends[k])
        def _(k=k):
            l_copies[k].wait_send()


def per_device(F, H, queries, key_vectors, value_vectors, frame_index, height_index, width_index, frame_block,
               conv_weight, conv_bias):
    FC, HG, W, C = queries.shape
    heads = C // HD
    assert FC == 2 and H % 2 == 0 and F % 2 == 0
    Y = H // 2
    T, TF, RD = FC * HG * W, HG * W, HG // H
    TD = RD * W
    O = conv_weight.shape[-1]
    chunks = [COLUMNS] * (O // COLUMNS) + ([O % COLUMNS] if O % COLUMNS else [])
    outer = max(F // 2 - 1, 1)
    down = (-(-(BLOCK_MOST - 1) // FC) + 1) // 2
    lanes = heads * PAD
    vmem = pl.BlockSpec(memory_space=pltpu.VMEM)
    dma = pltpu.SemaphoreType.DMA
    return pl.pallas_call(
        functools.partial(kernel, (F, Y, heads, HG, W, tuple(chunks))),
        out_shape=jax.ShapeDtypeStruct((RD, FC, W, O), BF16),
        in_specs=[pl.BlockSpec(memory_space=pl.ANY)] * 9,
        out_specs=vmem,
        scratch_shapes=[
            pltpu.VMEM((T, C), BF16),
            pltpu.VMEM((T, C), BF16),
            pltpu.VMEM((T, C), BF16),
            pltpu.SMEM((FC,), jnp.int32),
            pltpu.SMEM((HG,), jnp.int32),
            pltpu.SMEM((W,), jnp.int32),
            pltpu.SMEM((FC,), jnp.int32),
            pltpu.VMEM((O,), F32),
            dma((8,)),
            pltpu.VMEM((2,) + conv_weight.shape, BF16),
            pltpu.VMEM((T, C), BF16),
            pltpu.VMEM((16, lanes), F32),
            pltpu.VMEM((16, lanes), F32),
            *[pltpu.VMEM((lanes, PAD), BF16)] * 5,
            pltpu.VMEM((outer, lanes, PAD), BF16),
            pltpu.VMEM((down, lanes, PAD), BF16),
            *[pltpu.VMEM((lanes, PAD), BF16)] * 3,
            pltpu.VMEM((lanes, PAD), F32),
            pltpu.VMEM((4, lanes, PAD), F32),
            pltpu.VMEM((H, 2 + FC, TD, C), BF16),
            pltpu.VMEM((Y, 2 + FC, TD, C), BF16),
        ]
        + [pltpu.VMEM((max(Y - 1, 1), FC * TD, n), BF16) for n in chunks]
        + [pltpu.VMEM((max(Y - 1, 1), FC * TD, n), BF16) for n in chunks]
        + [pltpu.VMEM((FC * TD, n), F32) for n in chunks]
        + [
            dma, dma, dma, dma((2,)), dma((2,)),
            dma((outer,)), dma((outer,)), dma((down,)), dma((down,)), dma((3,)), dma((3,)),
            dma((Y,)), dma((Y,)),
            dma((max(Y - 1, 1) * len(chunks),)), dma((max(Y - 1, 1) * len(chunks),)),
        ],
        compiler_params=pltpu.CompilerParams(
            collective_id=0, has_side_effects=True, vmem_limit_bytes=60 * 1024 * 1024
        ),
        name="attend_conv",
    )(
        queries.reshape(T, C),
        key_vectors.reshape(T, C),
        value_vectors.reshape(T, C),
        frame_index,
        height_index,
        width_index,
        frame_block,
        conv_weight,
        conv_bias,
    )


def solution(mesh):
    placed = (
        P("frame", None, None, "head"),
        P("frame", None, None, "head"),
        P("frame", None, None, "head"),
        P("frame"),
        P(),
        P(),
        P("frame"),
        P(None, "head", None),
        P(),
    )
    return jax.shard_map(
        functools.partial(per_device, mesh.shape["frame"], mesh.shape["head"]),
        mesh=mesh,
        in_specs=placed,
        out_specs=P("head", "frame", None, None),
        check_vma=False,
    )
```

```python
import functools

import jax
import jax.numpy as jnp
import numpy as np
from jax import lax
from jax.experimental import pallas as pl
from jax.experimental.pallas import tpu as pltpu
from jax.sharding import PartitionSpec as P

HD = 112
PAD = 128
EPSILON = 1e-06
BLOCK_MOST = 6
COLUMNS = 512
F32 = jnp.float32
BF16 = jnp.bfloat16


def sections():
    side = HD * 5 // 14 // 2 * 2
    first = HD - 2 * side
    return ((0, first), (first, side), (first + side, side))


def tables(heads):
    C, lanes = heads * HD, heads * PAD
    lane = lax.broadcasted_iota(jnp.int32, (1, lanes), 1)
    head, d = lane // PAD, lane % PAD
    inside = d < HD
    source = jnp.where(inside, head * HD + d, -1)
    partner, sign = jnp.full_like(lane, -1), jnp.zeros((1, lanes), F32)
    freqs, masks = [], []
    for start, n in sections():
        half = n // 2
        low = (d >= start) & (d < start + half)
        high = (d >= start + half) & (d < start + n)
        partner = jnp.where(low, source + half, jnp.where(high, source - half, partner))
        sign = jnp.where(low, -1.0, jnp.where(high, 1.0, sign))
        j = jnp.where(low, d - start, d - start - half).astype(F32)
        either = low | high
        freqs.append(jnp.where(either, jnp.exp(j * float(-2.0 * np.log(10000.0) / n)), 0.0))
        masks.append(jnp.where(either, 1.0, 0.0))
    row = lax.broadcasted_iota(jnp.int32, (C, lanes), 0)
    spread = jnp.where(row == source, 1.0, 0.0).astype(BF16)
    swap = jnp.where(row == partner, sign, 0.0).astype(BF16)
    column = lax.broadcasted_iota(jnp.int32, (1, C), 1)
    target = column // HD * PAD + column % HD
    row = lax.broadcasted_iota(jnp.int32, (lanes, C), 0)
    gather = jnp.where(row == target, 1.0, 0.0).astype(BF16)
    return spread, swap, gather, freqs, masks


def positions(ref, count, rows, lanes):
    row = lax.broadcasted_iota(jnp.int32, (rows, lanes), 0)
    result = jnp.zeros((rows, lanes), F32)
    for i in range(count):
        result = jnp.where(row == i, ref[i].astype(F32), result)
    return result


def mm(a, b):
    return jnp.dot(a, b, preferred_element_type=F32)


def mm_t(a, b):
    return lax.dot_general(a, b, (((0,), (0,)), ((), ())), preferred_element_type=F32)


def mm_n(a, b):
    return lax.dot_general(a, b, (((1,), (1,)), ((), ())), preferred_element_type=F32)


def split(a):
    high = a.astype(BF16)
    return high, (a - high.astype(F32)).astype(BF16)


def kernel(
    cfg, q_any, k_any, v_any, fi_any, hi_any, wi_any, fb_any, w_ref, out_ref,
    q_ref, k_ref, v_ref, fi_ref, hi_ref, wi_ref, fb_ref, in_sem, w_buf, qh, q_relay, time_own, time_prev, msg_t, msg_l, msg_n, msg_r, msg_j, recv_t, recv_l, recv_n, recv_r, recv_j, base, state, att, att_x, *rest,
):
    F, Y, heads, HG, W, chunks = cfg
    n_chunk = len(chunks)
    part_send, part_recv, part_own = rest[:n_chunk], rest[n_chunk : 2 * n_chunk], rest[2 * n_chunk : 3 * n_chunk]
    (w_sem, w_send, w_recv, halo_send, halo_recv, t_send, t_recv, l_send, l_recv, p_send, p_recv,
          x_send, x_recv, c_send, c_recv) = rest[3 * n_chunk :]
    FC = 2
    H = 2 * Y
    TF = HG * W
    RD = HG // H
    TD = RD * W
    O = F // 2
    reach = -(-(BLOCK_MOST - 1) // FC)
    down = (reach + 1) // 2
    f = lax.axis_index("frame")
    h = lax.axis_index("head")
    y, c = h // 2, h % 2
    mate = 2 * y + (1 - c)
    inner, outer = f % 2, f // 2
    partner = f + 1 - 2 * inner

    loads = [
        pltpu.make_async_copy(src, dst, in_sem.at[i])
        for i, (src, dst) in enumerate(
            [(fi_any, fi_ref), (hi_any, hi_ref), (wi_any, wi_ref), (fb_any, fb_ref), (k_any, k_ref), (v_any, v_ref),
             (q_any, q_ref)]
        )
    ]
    for load in loads:
        load.start()

    barrier = pltpu.get_barrier_semaphore()
    for k in range(1, F):
        pl.semaphore_signal(barrier, inc=1, device_id=(lax.rem(f + k, F), h), device_id_type=pl.DeviceIdType.MESH)
    pl.semaphore_signal(barrier, inc=1, device_id=(f, mate), device_id_type=pl.DeviceIdType.MESH)
    for j in range(1, Y):
        pl.semaphore_signal(
            barrier, inc=1, device_id=(f, 2 * lax.rem(y + j, Y) + c), device_id_type=pl.DeviceIdType.MESH
        )

    def remote(src, dst, send, recv, frame, head):
        return pltpu.make_async_remote_copy(
            src_ref=src, dst_ref=dst, send_sem=send, recv_sem=recv,
            device_id=(frame, head), device_id_type=pl.DeviceIdType.MESH,
        )

    w_local = pltpu.make_async_copy(w_ref, w_buf.at[0], w_sem)
    w_local.start()

    lanes = heads * PAD
    spread, swap, gather, freqs, masks = tables(heads)
    for load in loads[:4]:
        load.wait()
    t_ang = positions(fi_ref, FC, 8, lanes) * freqs[0]
    time_own[0:8, :] = jnp.cos(t_ang) * masks[0]
    time_own[8:16, :] = jnp.sin(t_ang)
    h_ang = positions(hi_ref, HG, HG, lanes) * freqs[1]
    w_ang = positions(wi_ref, W, W, lanes) * freqs[2]
    cos_hw = (
        (jnp.cos(h_ang) * masks[1]).reshape(HG, 1, lanes) + (jnp.cos(w_ang) * masks[2]).reshape(1, W, lanes)
    ).reshape(TF, lanes)
    sin_hw = (jnp.sin(h_ang).reshape(HG, 1, lanes) + jnp.sin(w_ang).reshape(1, W, lanes)).reshape(TF, lanes)

    pl.semaphore_wait(barrier, (F - 1) + 1 + (Y - 1))

    w_far = remote(w_ref, w_buf.at[1], w_send, w_recv, f, mate)
    w_far.start()
    nxt = lax.rem(f + 1, F)
    first, second = pl.ds(0, TF), pl.ds(TF, TF)
    q_copy = remote(q_any.at[first], qh.at[first], halo_send.at[0], halo_recv.at[0], nxt, h)
    t_copy = remote(time_own, time_prev, halo_send.at[1], halo_recv.at[1], nxt, h)
    straight = remote(q_any.at[second], qh.at[second], halo_send.at[2], halo_recv.at[2], partner, h)
    detour = remote(q_any.at[second], q_relay, halo_send.at[3], halo_recv.at[3], lax.rem(f + 2, F), h)
    onward = remote(q_relay, qh.at[second], halo_send.at[2], halo_recv.at[2], partner, h)

    @pl.when(f < F - 1)
    def _():
        q_copy.start()
        t_copy.start()

    @pl.when(inner == 0)
    def _():
        straight.start()

    @pl.when((inner == 1) & (outer < O - 1))
    def _():
        detour.start()

    @pl.when(f == 0)
    def _():
        qh[...] = jnp.zeros_like(qh)
        time_prev[...] = jnp.zeros_like(time_prev)
        recv_n[...] = jnp.zeros_like(recv_n)


    def rotated(rows, cos_t, sin_t):
        positive = jnp.maximum(rows, jnp.zeros_like(rows))
        plain = mm(positive, spread)
        turned = mm(positive, swap)
        return plain.astype(BF16), plain * (cos_hw + cos_t) + turned * (sin_hw + sin_t)

    ones = jnp.where(lax.broadcasted_iota(jnp.int32, (PAD, TF), 0) >= HD, 1.0, 0.0).astype(BF16)
    for load in loads[4:6]:
        load.wait()
    frames = []
    for t in range(FC):
        rows = slice(t * TF, (t + 1) * TF)
        k_pos, k_rot = rotated(k_ref[rows, :], time_own[t : t + 1, :], time_own[8 + t : 9 + t, :])
        k_hi, k_lo = split(k_rot)
        value = mm(v_ref[rows, :], spread).astype(BF16)
        per_head = []
        totals = mm(ones, k_pos)
        for g in range(heads):
            cut = slice(g * PAD, (g + 1) * PAD)
            both = mm_t(value[:, cut], jnp.concatenate([k_hi[:, cut], k_lo[:, cut]], axis=1))
            per_head.append(both[:, :PAD] + both[:, PAD:] + totals[:, cut])
        frames.append(jnp.concatenate(per_head, axis=0))
    id0 = fb_ref[0].astype(F32)
    id1 = fb_ref[1].astype(F32)
    same = jnp.where(id0 == id1, 1.0, 0.0)
    own_t = frames[0] + frames[1]
    own_l = frames[0] + same * frames[1]
    row = lax.broadcasted_iota(jnp.int32, own_t.shape, 0)

    def tagged(value, first, second):
        return jnp.where(row == HD + 1, first, jnp.where(row == HD + 2, second, value)).astype(BF16)

    msg_t[...] = own_t.astype(BF16)
    msg_l[...] = tagged(own_l, id0, id1)
    msg_n[...] = tagged((same - 1.0) * frames[1], id0, id1)

    t_copies, l_copies, l_sends, l_gets = {}, {}, {}, {}
    for k in range(1, O):
        t_copies[k] = remote(
            msg_t, recv_t.at[k - 1], t_send.at[k - 1], t_recv.at[k - 1], lax.rem(f + 2 * k, F), h
        )
    for k in range(1, down + 1):
        l_copies[k] = remote(
            msg_l, recv_l.at[k - 1], l_send.at[k - 1], l_recv.at[k - 1], lax.rem(f - 2 * k + 2 * F, F), h
        )
        wanted = 2 * k <= reach + 1 - inner
        l_sends[k] = wanted & (outer >= k)
        l_gets[k] = wanted & (outer + k < O)
    n_copy = remote(msg_n, recv_n, p_send.at[0], p_recv.at[0], nxt, h)
    r_copy = remote(msg_r, recv_r, p_send.at[1], p_recv.at[1], partner, h)
    j_copy = remote(msg_j, recv_j, p_send.at[2], p_recv.at[2], partner, h)
    for k in range(O - 1, 0, -1):

        @pl.when(outer + k < O)
        def _(k=k):
            t_copies[k].start()

    for k in range(down, 0, -1):

        @pl.when(l_sends[k])
        def _(k=k):
            l_copies[k].start()

    @pl.when(f < F - 1)
    def _():
        n_copy.start()

    @pl.when((inner == 1) & (outer > 0))
    def _():
        detour.wait_recv()
        onward.start()

    loads[6].wait()
    q_parts = [None, None]
    for t in range(FC):
        rows = slice(t * TF, (t + 1) * TF)
        q_parts.append(rotated(q_ref[rows, :], time_own[t : t + 1, :], time_own[8 + t : 9 + t, :]))

    @pl.when(inner == 0)
    def _():
        base[...] = own_t

    @pl.when(inner == 1)
    def _():
        base[...] = jnp.zeros_like(own_t)

    for k in range(1, O):

        @pl.when(outer >= k)
        def _(k=k):
            t_copies[k].wait_recv()
            base[...] += recv_t[k - 1].astype(F32)

    msg_r[...] = base[...].astype(BF16)
    r_copy.start()

    for k in range(1, down + 1):

        @pl.when(l_gets[k])
        def _(k=k):
            l_copies[k].wait_recv()

        @pl.when(jnp.logical_not(l_gets[k]))
        def _(k=k):
            recv_l[k - 1] = tagged(jnp.zeros_like(own_t), -1.0, -1.0)

    def joined(ident, total, pieces):
        for piece in pieces:
            total = total + jnp.where(piece[HD + 1 : HD + 2] == ident, 1.0, 0.0) * piece
        return tagged(total, ident, ident)

    leads = [recv_l[k].astype(F32) for k in range(down)]

    @pl.when(inner == 0)
    def _():
        msg_j[...] = joined(leads[0][HD + 1 : HD + 2], leads[0], leads[1:])

    @pl.when(inner == 1)
    def _():
        msg_j[...] = joined(id0, own_l, leads[:1])

    j_copy.start()

    @pl.when(f > 0)
    def _():
        q_copy.wait_recv()
        t_copy.wait_recv()
        straight.wait_recv()

    for t in range(FC):
        rows = slice(t * TF, (t + 1) * TF)
        q_parts[t] = rotated(qh[rows, :], time_prev[t : t + 1, :], time_prev[8 + t : 9 + t, :])

    @pl.when(f > 0)
    def _():
        n_copy.wait_recv()

    r_copy.wait_recv()
    j_copy.wait_recv()
    before = base[...] + recv_r[...].astype(F32) - jnp.where(inner == 0, 1.0, 0.0) * own_t
    less = recv_n[...].astype(F32)
    tails = [recv_j[...].astype(F32)] + leads
    ids = [less[HD + 1 : HD + 2], less[HD + 2 : HD + 3], id0, id1]
    starts = [before + less, before, before + own_l, before + own_t]
    for i in range(2 + FC):
        total = starts[i]
        if i < 2:
            total = total + jnp.where(ids[i] == id0, 1.0, 0.0) * own_l
        for tail in tails:
            total = total + jnp.where(tail[HD + 1 : HD + 2] == ids[i], 1.0, 0.0) * tail
        state[i] = total

    x_copies = []
    for t in (2, 3, 0, 1):
        q_pos, q_rot = q_parts[t]
        q_hi, q_lo = split(q_rot)
        full = state[t]
        merged = []
        for g in range(heads):
            cut = slice(g * PAD, (g + 1) * PAD)
            block = full[cut, :]
            s_hi, s_lo = split(block)
            total_hi, total_lo = split(jnp.broadcast_to(block[HD : HD + 1, :], (PAD, PAD)))
            both = mm_n(q_hi[:, cut], jnp.concatenate([s_hi, s_lo], axis=0))
            numerator = both[:, :PAD] + both[:, PAD:] + mm_n(q_lo[:, cut], s_hi)
            both = mm_n(q_pos[:, cut], jnp.concatenate([total_hi, total_lo], axis=0))
            denominator = both[:, :PAD] + both[:, PAD:] + EPSILON
            merged.append((numerator / denominator).astype(BF16))
        tight = mm(jnp.concatenate(merged, axis=1), gather).astype(BF16)
        for g in range(H):
            att[g, t] = tight[g * TD : (g + 1) * TD]

        if t % 2 == 1:
            pair = pl.ds(t - 1, 2)
            for j in range(Y):
                slot = j if t == 3 else Y + j
                x_copies.append(
                    remote(att.at[2 * j + 1 - c, pair], att_x.at[j, pair], x_send.at[slot], x_recv.at[slot], f, mate)
                )
                x_copies[-1].start()

    starts = np.cumsum([0] + list(chunks))
    owners = [lax.rem(y + j, Y) for j in range(1, Y)] + [y]
    M = FC * TD

    def lhs(tap, side):
        rows = [(att.at[2 * j + c] if side == 0 else att_x.at[j])[2 - tap : 2 - tap + FC] for j in owners]
        return jnp.concatenate([r.reshape(M, heads * HD) for r in rows], axis=0)

    def product(taps, side, n):
        cols = slice(int(starts[n]), int(starts[n + 1]))
        total = None
        for tap in range(3):
            term = mm(taps[tap], w_buf[side, tap, :, cols])
            total = term if total is None else total + term
        return total

    w_local.wait()
    near = [lhs(tap, 0) for tap in range(3)]
    ahead = [product(near, 0, n) for n in range(min(2, n_chunk))]
    w_far.wait_recv()
    for copy in x_copies:
        copy.wait_recv()
    far = [lhs(tap, 1) for tap in range(3)]

    c_copies = {}
    for n in range(n_chunk):
        total = product(far, 1, n) + (ahead[n] if n < len(ahead) else product(near, 0, n))
        for j in range(1, Y):
            part_send[n][j - 1] = total[(j - 1) * M : j * M].astype(BF16)
            slot = (j - 1) * n_chunk + n
            c_copies[j, n] = remote(
                part_send[n].at[j - 1], part_recv[n].at[j - 1], c_send.at[slot], c_recv.at[slot], f,
                2 * owners[j - 1] + c,
            )
            c_copies[j, n].start()
        part_own[n][...] = total[(Y - 1) * M :]
    for n in range(n_chunk):
        cols = slice(int(starts[n]), int(starts[n + 1]))
        total = part_own[n][...]
        for j in range(1, Y):
            c_copies[j, n].wait_recv()
            total = total + part_recv[n][j - 1].astype(F32)
        for t in range(FC):
            for r in range(RD):
                start = t * TD + r * W
                out_ref[r, t, :, cols] = total[start : start + W]

    w_far.wait_send()
    for copy in x_copies + list(c_copies.values()):
        copy.wait_send()

    @pl.when(f < F - 1)
    def _():
        q_copy.wait_send()
        t_copy.wait_send()
        n_copy.wait_send()

    @pl.when(inner == 0)
    def _():
        straight.wait_send()

    @pl.when((inner == 1) & (outer < O - 1))
    def _():
        detour.wait_send()

    @pl.when((inner == 1) & (outer > 0))
    def _():
        onward.wait_send()

    r_copy.wait_send()
    j_copy.wait_send()
    for k in range(1, O):

        @pl.when(outer + k < O)
        def _(k=k):
            t_copies[k].wait_send()

    for k in range(1, down + 1):

        @pl.when(l_sends[k])
        def _(k=k):
            l_copies[k].wait_send()


def per_device(F, H, queries, key_vectors, value_vectors, frame_index, height_index, width_index, frame_block,
               conv_weight, conv_bias):
    FC, HG, W, C = queries.shape
    heads = C // HD
    assert FC == 2 and H % 2 == 0 and F % 2 == 0
    Y = H // 2
    T, TF, RD = FC * HG * W, HG * W, HG // H
    TD = RD * W
    O = conv_weight.shape[-1]
    chunks = [COLUMNS] * (O // COLUMNS) + ([O % COLUMNS] if O % COLUMNS else [])
    outer = max(F // 2 - 1, 1)
    down = (-(-(BLOCK_MOST - 1) // FC) + 1) // 2
    lanes = heads * PAD
    vmem = pl.BlockSpec(memory_space=pltpu.VMEM)
    dma = pltpu.SemaphoreType.DMA
    summed = pl.pallas_call(
        functools.partial(kernel, (F, Y, heads, HG, W, tuple(chunks))),
        out_shape=jax.ShapeDtypeStruct((RD, FC, W, O), F32),
        in_specs=[pl.BlockSpec(memory_space=pltpu.HBM)] * 8,
        out_specs=vmem,
        scratch_shapes=[
            pltpu.VMEM((T, C), BF16),
            pltpu.VMEM((T, C), BF16),
            pltpu.VMEM((T, C), BF16),
            pltpu.SMEM((FC,), jnp.int32),
            pltpu.SMEM((HG,), jnp.int32),
            pltpu.SMEM((W,), jnp.int32),
            pltpu.SMEM((FC,), jnp.int32),
            dma((7,)),
            pltpu.VMEM((2,) + conv_weight.shape, BF16),
            pltpu.VMEM((T, C), BF16),
            pltpu.VMEM((TF, C), BF16),
            pltpu.VMEM((16, lanes), F32),
            pltpu.VMEM((16, lanes), F32),
            *[pltpu.VMEM((lanes, PAD), BF16)] * 5,
            pltpu.VMEM((outer, lanes, PAD), BF16),
            pltpu.VMEM((down, lanes, PAD), BF16),
            *[pltpu.VMEM((lanes, PAD), BF16)] * 3,
            pltpu.VMEM((lanes, PAD), F32),
            pltpu.VMEM((4, lanes, PAD), F32),
            pltpu.VMEM((H, 2 + FC, TD, C), BF16),
            pltpu.VMEM((Y, 2 + FC, TD, C), BF16),
        ]
        + [pltpu.VMEM((max(Y - 1, 1), FC * TD, n), BF16) for n in chunks]
        + [pltpu.VMEM((max(Y - 1, 1), FC * TD, n), BF16) for n in chunks]
        + [pltpu.VMEM((FC * TD, n), F32) for n in chunks]
        + [
            dma, dma, dma, dma((4,)), dma((4,)),
            dma((outer,)), dma((outer,)), dma((down,)), dma((down,)), dma((3,)), dma((3,)),
            dma((2 * Y,)), dma((2 * Y,)),
            dma((max(Y - 1, 1) * len(chunks),)), dma((max(Y - 1, 1) * len(chunks),)),
        ],
        compiler_params=pltpu.CompilerParams(
            collective_id=0, has_side_effects=True, vmem_limit_bytes=60 * 1024 * 1024
        ),
        name="attend_conv",
    )(
        queries.reshape(T, C),
        key_vectors.reshape(T, C),
        value_vectors.reshape(T, C),
        frame_index,
        height_index,
        width_index,
        frame_block,
        conv_weight,
    )
    return jax.nn.silu(summed + conv_bias).astype(BF16)


def solution(mesh):
    placed = (
        P("frame", None, None, "head"),
        P("frame", None, None, "head"),
        P("frame", None, None, "head"),
        P("frame"),
        P(),
        P(),
        P("frame"),
        P(None, "head", None),
        P(),
    )
    return jax.shard_map(
        functools.partial(per_device, mesh.shape["frame"], mesh.shape["head"]),
        mesh=mesh,
        in_specs=placed,
        out_specs=P("head", "frame", None, None),
        check_vma=False,
    )
```

```python
import functools

import jax
import jax.numpy as jnp
import numpy as np
from jax import lax
from jax.experimental import pallas as pl
from jax.experimental.pallas import tpu as pltpu
from jax.sharding import PartitionSpec as P

HD = 112
PAD = 128
EPSILON = 1e-06
BLOCK_MOST = 6
COLUMNS = 512
F32 = jnp.float32
BF16 = jnp.bfloat16


def sections():
    side = HD * 5 // 14 // 2 * 2
    first = HD - 2 * side
    return ((0, first), (first, side), (first + side, side))


def tables(heads):
    C, lanes = heads * HD, heads * PAD
    lane = lax.broadcasted_iota(jnp.int32, (1, lanes), 1)
    head, d = lane // PAD, lane % PAD
    inside = d < HD
    source = jnp.where(inside, head * HD + d, -1)
    partner, sign = jnp.full_like(lane, -1), jnp.zeros((1, lanes), F32)
    freqs, masks = [], []
    for start, n in sections():
        half = n // 2
        low = (d >= start) & (d < start + half)
        high = (d >= start + half) & (d < start + n)
        partner = jnp.where(low, source + half, jnp.where(high, source - half, partner))
        sign = jnp.where(low, -1.0, jnp.where(high, 1.0, sign))
        j = jnp.where(low, d - start, d - start - half).astype(F32)
        either = low | high
        freqs.append(jnp.where(either, jnp.exp(j * float(-2.0 * np.log(10000.0) / n)), 0.0))
        masks.append(jnp.where(either, 1.0, 0.0))
    row = lax.broadcasted_iota(jnp.int32, (C, lanes), 0)
    spread = jnp.where(row == source, 1.0, 0.0).astype(BF16)
    swap = jnp.where(row == partner, sign, 0.0).astype(BF16)
    column = lax.broadcasted_iota(jnp.int32, (1, C), 1)
    target = column // HD * PAD + column % HD
    row = lax.broadcasted_iota(jnp.int32, (lanes, C), 0)
    gather = jnp.where(row == target, 1.0, 0.0).astype(BF16)
    return spread, swap, gather, freqs, masks


def positions(ref, count, rows, lanes):
    row = lax.broadcasted_iota(jnp.int32, (rows, lanes), 0)
    result = jnp.zeros((rows, lanes), F32)
    for i in range(count):
        result = jnp.where(row == i, ref[i].astype(F32), result)
    return result


def mm(a, b):
    return jnp.dot(a, b, preferred_element_type=F32)


def mm_t(a, b):
    return lax.dot_general(a, b, (((0,), (0,)), ((), ())), preferred_element_type=F32)


def mm_n(a, b):
    return lax.dot_general(a, b, (((1,), (1,)), ((), ())), preferred_element_type=F32)


def split(a):
    high = a.astype(BF16)
    return high, (a - high.astype(F32)).astype(BF16)


def kernel(
    cfg, q_any, k_any, v_any, fi_any, hi_any, wi_any, fb_any, w_ref, bias_any, out_ref,
    q_ref, k_ref, v_ref, fi_ref, hi_ref, wi_ref, fb_ref, bias_ref, in_sem, w_buf, qh, time_own, time_prev, msg_t, msg_l, msg_n, msg_r, msg_j, recv_t, recv_l, recv_n, recv_r, recv_j, base, state, att, att_x, *rest,
):
    F, Y, heads, HG, W, chunks = cfg
    n_chunk = len(chunks)
    part_send, part_recv, part_own = rest[:n_chunk], rest[n_chunk : 2 * n_chunk], rest[2 * n_chunk : 3 * n_chunk]
    (w_sem, w_send, w_recv, halo_send, halo_recv, t_send, t_recv, l_send, l_recv, p_send, p_recv,
          x_send, x_recv, c_send, c_recv) = rest[3 * n_chunk :]
    FC = 2
    H = 2 * Y
    TF = HG * W
    RD = HG // H
    TD = RD * W
    O = F // 2
    reach = -(-(BLOCK_MOST - 1) // FC)
    down = (reach + 1) // 2
    f = lax.axis_index("frame")
    h = lax.axis_index("head")
    y, c = h // 2, h % 2
    mate = 2 * y + (1 - c)
    inner, outer = f % 2, f // 2
    partner = f + 1 - 2 * inner

    loads = [
        pltpu.make_async_copy(src, dst, in_sem.at[i])
        for i, (src, dst) in enumerate(
            [(fi_any, fi_ref), (hi_any, hi_ref), (wi_any, wi_ref), (fb_any, fb_ref), (k_any, k_ref), (v_any, v_ref),
             (q_any, q_ref), (bias_any, bias_ref)]
        )
    ]
    for load in loads:
        load.start()

    barrier = pltpu.get_barrier_semaphore()
    for k in range(1, F):
        pl.semaphore_signal(barrier, inc=1, device_id=(lax.rem(f + k, F), h), device_id_type=pl.DeviceIdType.MESH)
    pl.semaphore_signal(barrier, inc=1, device_id=(f, mate), device_id_type=pl.DeviceIdType.MESH)
    for j in range(1, Y):
        pl.semaphore_signal(
            barrier, inc=1, device_id=(f, 2 * lax.rem(y + j, Y) + c), device_id_type=pl.DeviceIdType.MESH
        )

    def remote(src, dst, send, recv, frame, head):
        return pltpu.make_async_remote_copy(
            src_ref=src, dst_ref=dst, send_sem=send, recv_sem=recv,
            device_id=(frame, head), device_id_type=pl.DeviceIdType.MESH,
        )

    w_local = pltpu.make_async_copy(w_ref, w_buf.at[0], w_sem)
    w_local.start()

    lanes = heads * PAD
    spread, swap, gather, freqs, masks = tables(heads)
    for load in loads[:4]:
        load.wait()
    t_ang = positions(fi_ref, FC, 8, lanes) * freqs[0]
    time_own[0:8, :] = jnp.cos(t_ang) * masks[0]
    time_own[8:16, :] = jnp.sin(t_ang)
    h_ang = positions(hi_ref, HG, HG, lanes) * freqs[1]
    w_ang = positions(wi_ref, W, W, lanes) * freqs[2]
    cos_hw = (
        (jnp.cos(h_ang) * masks[1]).reshape(HG, 1, lanes) + (jnp.cos(w_ang) * masks[2]).reshape(1, W, lanes)
    ).reshape(TF, lanes)
    sin_hw = (jnp.sin(h_ang).reshape(HG, 1, lanes) + jnp.sin(w_ang).reshape(1, W, lanes)).reshape(TF, lanes)

    pl.semaphore_wait(barrier, (F - 1) + 1 + (Y - 1))

    w_far = remote(w_ref, w_buf.at[1], w_send, w_recv, f, mate)
    nxt = lax.rem(f + 1, F)
    q_copy = remote(q_any, qh, halo_send.at[0], halo_recv.at[0], nxt, h)
    t_copy = remote(time_own, time_prev, halo_send.at[1], halo_recv.at[1], nxt, h)

    @pl.when(f < F - 1)
    def _():
        q_copy.start()
        t_copy.start()

    @pl.when(f == 0)
    def _():
        qh[...] = jnp.zeros_like(qh)
        time_prev[...] = jnp.zeros_like(time_prev)
        recv_n[...] = jnp.zeros_like(recv_n)


    def rotated(rows, cos_t, sin_t):
        positive = jnp.maximum(rows, jnp.zeros_like(rows))
        plain = mm(positive, spread)
        turned = mm(positive, swap)
        return plain.astype(BF16), plain * (cos_hw + cos_t) + turned * (sin_hw + sin_t)

    ones = jnp.where(lax.broadcasted_iota(jnp.int32, (PAD, TF), 0) >= HD, 1.0, 0.0).astype(BF16)
    for load in loads[4:6]:
        load.wait()
    frames = []
    for t in range(FC):
        rows = slice(t * TF, (t + 1) * TF)
        k_pos, k_rot = rotated(k_ref[rows, :], time_own[t : t + 1, :], time_own[8 + t : 9 + t, :])
        k_hi, k_lo = split(k_rot)
        value = mm(v_ref[rows, :], spread).astype(BF16)
        per_head = []
        totals = mm(ones, k_pos)
        for g in range(heads):
            cut = slice(g * PAD, (g + 1) * PAD)
            both = mm_t(value[:, cut], jnp.concatenate([k_hi[:, cut], k_lo[:, cut]], axis=1))
            per_head.append(both[:, :PAD] + both[:, PAD:] + totals[:, cut])
        frames.append(jnp.concatenate(per_head, axis=0))
    id0 = fb_ref[0].astype(F32)
    id1 = fb_ref[1].astype(F32)
    same = jnp.where(id0 == id1, 1.0, 0.0)
    own_t = frames[0] + frames[1]
    own_l = frames[0] + same * frames[1]
    row = lax.broadcasted_iota(jnp.int32, own_t.shape, 0)

    def tagged(value, first, second):
        return jnp.where(row == HD + 1, first, jnp.where(row == HD + 2, second, value)).astype(BF16)

    msg_t[...] = own_t.astype(BF16)
    msg_l[...] = tagged(own_l, id0, id1)
    msg_n[...] = tagged((same - 1.0) * frames[1], id0, id1)

    t_copies, l_copies, l_sends, l_gets = {}, {}, {}, {}
    for k in range(1, O):
        t_copies[k] = remote(
            msg_t, recv_t.at[k - 1], t_send.at[k - 1], t_recv.at[k - 1], lax.rem(f + 2 * k, F), h
        )
    for k in range(1, down + 1):
        l_copies[k] = remote(
            msg_l, recv_l.at[k - 1], l_send.at[k - 1], l_recv.at[k - 1], lax.rem(f - 2 * k + 2 * F, F), h
        )
        wanted = 2 * k <= reach + 1 - inner
        l_sends[k] = wanted & (outer >= k)
        l_gets[k] = wanted & (outer + k < O)
    n_copy = remote(msg_n, recv_n, p_send.at[0], p_recv.at[0], nxt, h)
    r_copy = remote(msg_r, recv_r, p_send.at[1], p_recv.at[1], partner, h)
    j_copy = remote(msg_j, recv_j, p_send.at[2], p_recv.at[2], partner, h)
    @pl.when(f < F - 1)
    def _():
        n_copy.start()

    for k in range(O - 1, 0, -1):

        @pl.when(outer + k < O)
        def _(k=k):
            t_copies[k].start()

    for k in range(down, 0, -1):

        @pl.when(l_sends[k])
        def _(k=k):
            l_copies[k].start()

    w_far.start()

    loads[6].wait()
    q_parts = [None, None]
    for t in range(FC):
        rows = slice(t * TF, (t + 1) * TF)
        q_parts.append(rotated(q_ref[rows, :], time_own[t : t + 1, :], time_own[8 + t : 9 + t, :]))

    @pl.when(inner == 0)
    def _():
        base[...] = own_t

    @pl.when(inner == 1)
    def _():
        base[...] = jnp.zeros_like(own_t)

    for k in range(1, O):

        @pl.when(outer >= k)
        def _(k=k):
            t_copies[k].wait_recv()
            base[...] += recv_t[k - 1].astype(F32)

    msg_r[...] = base[...].astype(BF16)
    r_copy.start()

    for k in range(1, down + 1):

        @pl.when(l_gets[k])
        def _(k=k):
            l_copies[k].wait_recv()

        @pl.when(jnp.logical_not(l_gets[k]))
        def _(k=k):
            recv_l[k - 1] = tagged(jnp.zeros_like(own_t), -1.0, -1.0)

    def joined(ident, total, pieces):
        for piece in pieces:
            total = total + jnp.where(piece[HD + 1 : HD + 2] == ident, 1.0, 0.0) * piece
        return tagged(total, ident, ident)

    leads = [recv_l[k].astype(F32) for k in range(down)]

    @pl.when(inner == 0)
    def _():
        msg_j[...] = joined(leads[0][HD + 1 : HD + 2], leads[0], leads[1:])

    @pl.when(inner == 1)
    def _():
        msg_j[...] = joined(id0, own_l, leads[:1])

    j_copy.start()

    @pl.when(f > 0)
    def _():
        q_copy.wait_recv()
        t_copy.wait_recv()

    for t in range(FC):
        rows = slice(t * TF, (t + 1) * TF)
        q_parts[t] = rotated(qh[rows, :], time_prev[t : t + 1, :], time_prev[8 + t : 9 + t, :])

    @pl.when(f > 0)
    def _():
        n_copy.wait_recv()

    r_copy.wait_recv()
    j_copy.wait_recv()
    before = base[...] + recv_r[...].astype(F32) - jnp.where(inner == 0, 1.0, 0.0) * own_t
    less = recv_n[...].astype(F32)
    tails = [recv_j[...].astype(F32)] + leads
    ids = [less[HD + 1 : HD + 2], less[HD + 2 : HD + 3], id0, id1]
    starts = [before + less, before, before + own_l, before + own_t]
    for i in range(2 + FC):
        total = starts[i]
        if i < 2:
            total = total + jnp.where(ids[i] == id0, 1.0, 0.0) * own_l
        for tail in tails:
            total = total + jnp.where(tail[HD + 1 : HD + 2] == ids[i], 1.0, 0.0) * tail
        state[i] = total

    for t in range(2 + FC):
        q_pos, q_rot = q_parts[t]
        q_hi, q_lo = split(q_rot)
        full = state[t]
        merged = []
        for g in range(heads):
            cut = slice(g * PAD, (g + 1) * PAD)
            block = full[cut, :]
            s_hi, s_lo = split(block)
            total_hi, total_lo = split(jnp.broadcast_to(block[HD : HD + 1, :], (PAD, PAD)))
            both = mm_n(q_hi[:, cut], jnp.concatenate([s_hi, s_lo], axis=0))
            numerator = both[:, :PAD] + both[:, PAD:] + mm_n(q_lo[:, cut], s_hi)
            both = mm_n(q_pos[:, cut], jnp.concatenate([total_hi, total_lo], axis=0))
            denominator = both[:, :PAD] + both[:, PAD:] + EPSILON
            merged.append((numerator / denominator).astype(BF16))
        tight = mm(jnp.concatenate(merged, axis=1), gather).astype(BF16)
        for g in range(H):
            att[g, t] = tight[g * TD : (g + 1) * TD]

    x_copies = []
    for j in range(Y):
        x_copies.append(remote(att.at[2 * j + 1 - c], att_x.at[j], x_send.at[j], x_recv.at[j], f, mate))
        x_copies[-1].start()
    w_local.wait()
    w_far.wait_recv()
    for copy in x_copies:
        copy.wait_recv()

    starts = np.cumsum([0] + list(chunks))
    owners = [lax.rem(y + j, Y) for j in range(1, Y)] + [y]
    M = FC * TD
    taps = []
    for tap in range(3):
        for side in range(2):
            rows = [(att.at[2 * j + c] if side == 0 else att_x.at[j])[2 - tap : 2 - tap + FC] for j in owners]
            taps.append((tap, side, jnp.concatenate([r.reshape(M, heads * HD) for r in rows], axis=0)))

    c_copies = {}
    for n in range(n_chunk):
        cols = slice(int(starts[n]), int(starts[n + 1]))
        total = None
        for tap, side, rows in taps:
            term = mm(rows, w_buf[side, tap, :, cols])
            total = term if total is None else total + term
        for j in range(1, Y):
            part_send[n][j - 1] = total[(j - 1) * M : j * M].astype(BF16)
            slot = (j - 1) * n_chunk + n
            c_copies[j, n] = remote(
                part_send[n].at[j - 1], part_recv[n].at[j - 1], c_send.at[slot], c_recv.at[slot], f,
                2 * owners[j - 1] + c,
            )
            c_copies[j, n].start()
        part_own[n][...] = total[(Y - 1) * M :]
    loads[7].wait()
    bias = bias_ref[...].reshape(1, -1)
    for n in range(n_chunk):
        cols = slice(int(starts[n]), int(starts[n + 1]))
        total = part_own[n][...]
        for j in range(1, Y):
            c_copies[j, n].wait_recv()
            total = total + part_recv[n][j - 1].astype(F32)
        total = total + bias[:, cols]
        result = (total / (1.0 + jnp.exp(-total))).astype(BF16)
        for t in range(FC):
            for r in range(RD):
                start = t * TD + r * W
                out_ref[r, t, :, cols] = result[start : start + W]

    w_far.wait_send()
    for copy in x_copies + list(c_copies.values()):
        copy.wait_send()

    @pl.when(f < F - 1)
    def _():
        q_copy.wait_send()
        t_copy.wait_send()
        n_copy.wait_send()

    r_copy.wait_send()
    j_copy.wait_send()
    for k in range(1, O):

        @pl.when(outer + k < O)
        def _(k=k):
            t_copies[k].wait_send()

    for k in range(1, down + 1):

        @pl.when(l_sends[k])
        def _(k=k):
            l_copies[k].wait_send()


def per_device(F, H, queries, key_vectors, value_vectors, frame_index, height_index, width_index, frame_block,
               conv_weight, conv_bias):
    FC, HG, W, C = queries.shape
    heads = C // HD
    assert FC == 2 and H % 2 == 0 and F % 2 == 0
    Y = H // 2
    T, TF, RD = FC * HG * W, HG * W, HG // H
    TD = RD * W
    O = conv_weight.shape[-1]
    chunks = [COLUMNS] * (O // COLUMNS) + ([O % COLUMNS] if O % COLUMNS else [])
    outer = max(F // 2 - 1, 1)
    down = (-(-(BLOCK_MOST - 1) // FC) + 1) // 2
    lanes = heads * PAD
    vmem = pl.BlockSpec(memory_space=pltpu.VMEM)
    dma = pltpu.SemaphoreType.DMA
    return pl.pallas_call(
        functools.partial(kernel, (F, Y, heads, HG, W, tuple(chunks))),
        out_shape=jax.ShapeDtypeStruct((RD, FC, W, O), BF16),
        in_specs=[pl.BlockSpec(memory_space=pl.ANY)] * 9,
        out_specs=vmem,
        scratch_shapes=[
            pltpu.VMEM((T, C), BF16),
            pltpu.VMEM((T, C), BF16),
            pltpu.VMEM((T, C), BF16),
            pltpu.SMEM((FC,), jnp.int32),
            pltpu.SMEM((HG,), jnp.int32),
            pltpu.SMEM((W,), jnp.int32),
            pltpu.SMEM((FC,), jnp.int32),
            pltpu.VMEM((O,), F32),
            dma((8,)),
            pltpu.VMEM((2,) + conv_weight.shape, BF16),
            pltpu.VMEM((T, C), BF16),
            pltpu.VMEM((16, lanes), F32),
            pltpu.VMEM((16, lanes), F32),
            *[pltpu.VMEM((lanes, PAD), BF16)] * 5,
            pltpu.VMEM((outer, lanes, PAD), BF16),
            pltpu.VMEM((down, lanes, PAD), BF16),
            *[pltpu.VMEM((lanes, PAD), BF16)] * 3,
            pltpu.VMEM((lanes, PAD), F32),
            pltpu.VMEM((4, lanes, PAD), F32),
            pltpu.VMEM((H, 2 + FC, TD, C), BF16),
            pltpu.VMEM((Y, 2 + FC, TD, C), BF16),
        ]
        + [pltpu.VMEM((max(Y - 1, 1), FC * TD, n), BF16) for n in chunks]
        + [pltpu.VMEM((max(Y - 1, 1), FC * TD, n), BF16) for n in chunks]
        + [pltpu.VMEM((FC * TD, n), F32) for n in chunks]
        + [
            dma, dma, dma, dma((2,)), dma((2,)),
            dma((outer,)), dma((outer,)), dma((down,)), dma((down,)), dma((3,)), dma((3,)),
            dma((Y,)), dma((Y,)),
            dma((max(Y - 1, 1) * len(chunks),)), dma((max(Y - 1, 1) * len(chunks),)),
        ],
        compiler_params=pltpu.CompilerParams(
            collective_id=0, has_side_effects=True, vmem_limit_bytes=60 * 1024 * 1024
        ),
        name="attend_conv",
    )(
        queries.reshape(T, C),
        key_vectors.reshape(T, C),
        value_vectors.reshape(T, C),
        frame_index,
        height_index,
        width_index,
        frame_block,
        conv_weight,
        conv_bias,
    )


def solution(mesh):
    placed = (
        P("frame", None, None, "head"),
        P("frame", None, None, "head"),
        P("frame", None, None, "head"),
        P("frame"),
        P(),
        P(),
        P("frame"),
        P(None, "head", None),
        P(),
    )
    return jax.shard_map(
        functools.partial(per_device, mesh.shape["frame"], mesh.shape["head"]),
        mesh=mesh,
        in_specs=placed,
        out_specs=P("head", "frame", None, None),
        check_vma=False,
    )
```

```python
import functools

import jax
import jax.numpy as jnp
import numpy as np
from jax import lax
from jax.experimental import pallas as pl
from jax.experimental.pallas import tpu as pltpu
from jax.sharding import PartitionSpec as P

HD = 112
PAD = 128
EPSILON = 1e-06
BLOCK_MOST = 6
COLUMNS = 512
F32 = jnp.float32
BF16 = jnp.bfloat16


def sections():
    side = HD * 5 // 14 // 2 * 2
    first = HD - 2 * side
    return ((0, first), (first, side), (first + side, side))


def tables(heads):
    C, lanes = heads * HD, heads * PAD
    lane = lax.broadcasted_iota(jnp.int32, (1, lanes), 1)
    head, d = lane // PAD, lane % PAD
    inside = d < HD
    source = jnp.where(inside, head * HD + d, -1)
    partner, sign = jnp.full_like(lane, -1), jnp.zeros((1, lanes), F32)
    freqs, masks = [], []
    for start, n in sections():
        half = n // 2
        low = (d >= start) & (d < start + half)
        high = (d >= start + half) & (d < start + n)
        partner = jnp.where(low, source + half, jnp.where(high, source - half, partner))
        sign = jnp.where(low, -1.0, jnp.where(high, 1.0, sign))
        j = jnp.where(low, d - start, d - start - half).astype(F32)
        either = low | high
        freqs.append(jnp.where(either, jnp.exp(j * float(-2.0 * np.log(10000.0) / n)), 0.0))
        masks.append(jnp.where(either, 1.0, 0.0))
    row = lax.broadcasted_iota(jnp.int32, (C, lanes), 0)
    spread = jnp.where(row == source, 1.0, 0.0).astype(BF16)
    swap = jnp.where(row == partner, sign, 0.0).astype(BF16)
    column = lax.broadcasted_iota(jnp.int32, (1, C), 1)
    target = column // HD * PAD + column % HD
    row = lax.broadcasted_iota(jnp.int32, (lanes, C), 0)
    gather = jnp.where(row == target, 1.0, 0.0).astype(BF16)
    return spread, swap, gather, freqs, masks


def positions(ref, count, rows, lanes):
    row = lax.broadcasted_iota(jnp.int32, (rows, lanes), 0)
    result = jnp.zeros((rows, lanes), F32)
    for i in range(count):
        result = jnp.where(row == i, ref[i].astype(F32), result)
    return result


def mm(a, b):
    return jnp.dot(a, b, preferred_element_type=F32)


def mm_t(a, b):
    return lax.dot_general(a, b, (((0,), (0,)), ((), ())), preferred_element_type=F32)


def mm_n(a, b):
    return lax.dot_general(a, b, (((1,), (1,)), ((), ())), preferred_element_type=F32)


def split(a):
    high = a.astype(BF16)
    return high, (a - high.astype(F32)).astype(BF16)


def kernel(
    cfg, q_any, k_any, v_any, fi_any, hi_any, wi_any, fb_any, w_ref, bias_any, out_ref,
    q_ref, k_ref, v_ref, fi_ref, hi_ref, wi_ref, fb_ref, bias_ref, in_sem, w_buf, qh, time_own, time_prev, msg_t, msg_l, msg_n, msg_r, msg_j, recv_t, recv_l, recv_n, recv_r, recv_j, base, state, att, att_x, *rest,
):
    F, Y, heads, HG, W, chunks = cfg
    n_chunk = len(chunks)
    part_send, part_recv, part_own = rest[:n_chunk], rest[n_chunk : 2 * n_chunk], rest[2 * n_chunk : 3 * n_chunk]
    (w_sem, w_send, w_recv, halo_send, halo_recv, t_send, t_recv, l_send, l_recv, p_send, p_recv,
          x_send, x_recv, c_send, c_recv) = rest[3 * n_chunk :]
    FC = 2
    H = 2 * Y
    TF = HG * W
    RD = HG // H
    TD = RD * W
    O = F // 2
    reach = -(-(BLOCK_MOST - 1) // FC)
    down = (reach + 1) // 2
    f = lax.axis_index("frame")
    h = lax.axis_index("head")
    y, c = h // 2, h % 2
    mate = 2 * y + (1 - c)
    inner, outer = f % 2, f // 2
    partner = f + 1 - 2 * inner

    loads = [
        pltpu.make_async_copy(src, dst, in_sem.at[i])
        for i, (src, dst) in enumerate(
            [(fi_any, fi_ref), (hi_any, hi_ref), (wi_any, wi_ref), (fb_any, fb_ref), (k_any, k_ref), (v_any, v_ref),
             (q_any, q_ref), (bias_any, bias_ref)]
        )
    ]
    for load in loads:
        load.start()

    barrier = pltpu.get_barrier_semaphore()
    for k in range(1, F):
        pl.semaphore_signal(barrier, inc=1, device_id=(lax.rem(f + k, F), h), device_id_type=pl.DeviceIdType.MESH)
    pl.semaphore_signal(barrier, inc=1, device_id=(f, mate), device_id_type=pl.DeviceIdType.MESH)
    for j in range(1, Y):
        pl.semaphore_signal(
            barrier, inc=1, device_id=(f, 2 * lax.rem(y + j, Y) + c), device_id_type=pl.DeviceIdType.MESH
        )

    def remote(src, dst, send, recv, frame, head):
        return pltpu.make_async_remote_copy(
            src_ref=src, dst_ref=dst, send_sem=send, recv_sem=recv,
            device_id=(frame, head), device_id_type=pl.DeviceIdType.MESH,
        )

    w_local = pltpu.make_async_copy(w_ref, w_buf.at[0], w_sem)
    w_local.start()

    pl.semaphore_wait(barrier, (F - 1) + 1 + (Y - 1))

    w_far = remote(w_ref, w_buf.at[1], w_send, w_recv, f, mate)
    nxt = lax.rem(f + 1, F)
    q_copy = remote(q_any, qh, halo_send.at[0], halo_recv.at[0], nxt, h)
    t_copy = remote(time_own, time_prev, halo_send.at[1], halo_recv.at[1], nxt, h)

    @pl.when(f < F - 1)
    def _():
        q_copy.start()

    lanes = heads * PAD
    spread, swap, gather, freqs, masks = tables(heads)
    for load in loads[:4]:
        load.wait()
    t_ang = positions(fi_ref, FC, 8, lanes) * freqs[0]
    time_own[0:8, :] = jnp.cos(t_ang) * masks[0]
    time_own[8:16, :] = jnp.sin(t_ang)
    h_ang = positions(hi_ref, HG, HG, lanes) * freqs[1]
    w_ang = positions(wi_ref, W, W, lanes) * freqs[2]
    cos_hw = (
        (jnp.cos(h_ang) * masks[1]).reshape(HG, 1, lanes) + (jnp.cos(w_ang) * masks[2]).reshape(1, W, lanes)
    ).reshape(TF, lanes)
    sin_hw = (jnp.sin(h_ang).reshape(HG, 1, lanes) + jnp.sin(w_ang).reshape(1, W, lanes)).reshape(TF, lanes)

    @pl.when(f < F - 1)
    def _():
        t_copy.start()

    @pl.when(f == 0)
    def _():
        qh[...] = jnp.zeros_like(qh)
        time_prev[...] = jnp.zeros_like(time_prev)
        recv_n[...] = jnp.zeros_like(recv_n)


    def rotated(rows, cos_t, sin_t):
        positive = jnp.maximum(rows, jnp.zeros_like(rows))
        plain = mm(positive, spread)
        turned = mm(positive, swap)
        return plain.astype(BF16), plain * (cos_hw + cos_t) + turned * (sin_hw + sin_t)

    ones = jnp.where(lax.broadcasted_iota(jnp.int32, (PAD, TF), 0) >= HD, 1.0, 0.0).astype(BF16)
    for load in loads[4:6]:
        load.wait()
    frames = []
    for t in range(FC):
        rows = slice(t * TF, (t + 1) * TF)
        k_pos, k_rot = rotated(k_ref[rows, :], time_own[t : t + 1, :], time_own[8 + t : 9 + t, :])
        k_hi, k_lo = split(k_rot)
        value = mm(v_ref[rows, :], spread).astype(BF16)
        per_head = []
        totals = mm(ones, k_pos)
        for g in range(heads):
            cut = slice(g * PAD, (g + 1) * PAD)
            both = mm_t(value[:, cut], jnp.concatenate([k_hi[:, cut], k_lo[:, cut]], axis=1))
            per_head.append(both[:, :PAD] + both[:, PAD:] + totals[:, cut])
        frames.append(jnp.concatenate(per_head, axis=0))
    id0 = fb_ref[0].astype(F32)
    id1 = fb_ref[1].astype(F32)
    same = jnp.where(id0 == id1, 1.0, 0.0)
    own_t = frames[0] + frames[1]
    own_l = frames[0] + same * frames[1]
    row = lax.broadcasted_iota(jnp.int32, own_t.shape, 0)

    def tagged(value, first, second):
        return jnp.where(row == HD + 1, first, jnp.where(row == HD + 2, second, value)).astype(BF16)

    msg_t[0] = own_t.astype(BF16)
    msg_l[...] = tagged(own_l, id0, id1)
    msg_n[...] = tagged((same - 1.0) * frames[1], id0, id1)

    t_copies, l_copies, l_sends, l_gets = {}, {}, {}, {}
    steps = (O - 1).bit_length()
    for i in range(steps):
        for k in range(1, 2**i + 1):
            t_copies[i, k] = remote(
                msg_t.at[i], recv_t.at[i], t_send.at[2**i + k - 2], t_recv.at[i], lax.rem(f + 2 * k, F), h
            )

    def t_sends(i, k):
        return (outer % 2 ** (i + 1) == 2**i - 1) & (outer + k < O)

    def t_start(i):
        for k in range(2**i, 0, -1):

            @pl.when(t_sends(i, k))
            def _(k=k):
                t_copies[i, k].start()

    for k in range(1, down + 1):
        l_copies[k] = remote(
            msg_l, recv_l.at[k - 1], l_send.at[k - 1], l_recv.at[k - 1], lax.rem(f - 2 * k + 2 * F, F), h
        )
        wanted = 2 * k <= reach + 1 - inner
        l_sends[k] = wanted & (outer >= k)
        l_gets[k] = wanted & (outer + k < O)
    n_copy = remote(msg_n, recv_n, p_send.at[0], p_recv.at[0], nxt, h)
    r_copy = remote(msg_r, recv_r, p_send.at[1], p_recv.at[1], partner, h)
    j_copy = remote(msg_j, recv_j, p_send.at[2], p_recv.at[2], partner, h)
    @pl.when(f < F - 1)
    def _():
        n_copy.start()

    t_start(0)

    for k in range(down, 0, -1):

        @pl.when(l_sends[k])
        def _(k=k):
            l_copies[k].start()

    w_far.start()

    loads[6].wait()
    q_parts = [None, None]
    for t in range(FC):
        rows = slice(t * TF, (t + 1) * TF)
        q_parts.append(rotated(q_ref[rows, :], time_own[t : t + 1, :], time_own[8 + t : 9 + t, :]))

    base[...] = jnp.zeros_like(own_t)
    for i in range(steps):

        @pl.when(outer // 2**i % 2 == 1)
        def _(i=i):
            t_copies[i, 1].wait_recv()
            base[...] += recv_t[i].astype(F32)

        if i + 1 < steps:
            msg_t[i + 1] = (base[...] + own_t).astype(BF16)
            t_start(i + 1)

    earlier = base[...]
    msg_r[...] = (earlier + jnp.where(inner == 0, 1.0, 0.0) * own_t).astype(BF16)
    r_copy.start()

    for k in range(1, down + 1):

        @pl.when(l_gets[k])
        def _(k=k):
            l_copies[k].wait_recv()

        @pl.when(jnp.logical_not(l_gets[k]))
        def _(k=k):
            recv_l[k - 1] = tagged(jnp.zeros_like(own_t), -1.0, -1.0)

    def joined(ident, total, pieces):
        for piece in pieces:
            total = total + jnp.where(piece[HD + 1 : HD + 2] == ident, 1.0, 0.0) * piece
        return tagged(total, ident, ident)

    leads = [recv_l[k].astype(F32) for k in range(down)]

    @pl.when(inner == 0)
    def _():
        msg_j[...] = joined(leads[0][HD + 1 : HD + 2], leads[0], leads[1:])

    @pl.when(inner == 1)
    def _():
        msg_j[...] = joined(id0, own_l, leads[:1])

    j_copy.start()

    @pl.when(f > 0)
    def _():
        q_copy.wait_recv()
        t_copy.wait_recv()

    for t in range(FC):
        rows = slice(t * TF, (t + 1) * TF)
        q_parts[t] = rotated(qh[rows, :], time_prev[t : t + 1, :], time_prev[8 + t : 9 + t, :])

    @pl.when(f > 0)
    def _():
        n_copy.wait_recv()

    r_copy.wait_recv()
    j_copy.wait_recv()
    before = earlier + recv_r[...].astype(F32)
    less = recv_n[...].astype(F32)
    tails = [recv_j[...].astype(F32)] + leads
    ids = [less[HD + 1 : HD + 2], less[HD + 2 : HD + 3], id0, id1]
    starts = [before + less, before, before + own_l, before + own_t]
    for i in range(2 + FC):
        total = starts[i]
        if i < 2:
            total = total + jnp.where(ids[i] == id0, 1.0, 0.0) * own_l
        for tail in tails:
            total = total + jnp.where(tail[HD + 1 : HD + 2] == ids[i], 1.0, 0.0) * tail
        state[i] = total

    for t in range(2 + FC):
        q_pos, q_rot = q_parts[t]
        q_hi, q_lo = split(q_rot)
        full = state[t]
        merged = []
        for g in range(heads):
            cut = slice(g * PAD, (g + 1) * PAD)
            block = full[cut, :]
            s_hi, s_lo = split(block)
            total_hi, total_lo = split(jnp.broadcast_to(block[HD : HD + 1, :], (PAD, PAD)))
            both = mm_n(q_hi[:, cut], jnp.concatenate([s_hi, s_lo], axis=0))
            numerator = both[:, :PAD] + both[:, PAD:] + mm_n(q_lo[:, cut], s_hi)
            both = mm_n(q_pos[:, cut], jnp.concatenate([total_hi, total_lo], axis=0))
            denominator = both[:, :PAD] + both[:, PAD:] + EPSILON
            merged.append((numerator / denominator).astype(BF16))
        tight = mm(jnp.concatenate(merged, axis=1), gather).astype(BF16)
        for g in range(H):
            att[g, t] = tight[g * TD : (g + 1) * TD]

    x_copies = []
    for j in range(Y):
        x_copies.append(remote(att.at[2 * j + 1 - c], att_x.at[j], x_send.at[j], x_recv.at[j], f, mate))
        x_copies[-1].start()
    w_local.wait()
    w_far.wait_recv()
    for copy in x_copies:
        copy.wait_recv()

    starts = np.cumsum([0] + list(chunks))
    owners = [lax.rem(y + j, Y) for j in range(1, Y)] + [y]
    M = FC * TD
    taps = []
    for tap in range(3):
        for side in range(2):
            rows = [(att.at[2 * j + c] if side == 0 else att_x.at[j])[2 - tap : 2 - tap + FC] for j in owners]
            taps.append((tap, side, jnp.concatenate([r.reshape(M, heads * HD) for r in rows], axis=0)))

    c_copies = {}
    for n in range(n_chunk):
        cols = slice(int(starts[n]), int(starts[n + 1]))
        total = None
        for tap, side, rows in taps:
            term = mm(rows, w_buf[side, tap, :, cols])
            total = term if total is None else total + term
        for j in range(1, Y):
            part_send[n][j - 1] = total[(j - 1) * M : j * M].astype(BF16)
            slot = (j - 1) * n_chunk + n
            c_copies[j, n] = remote(
                part_send[n].at[j - 1], part_recv[n].at[j - 1], c_send.at[slot], c_recv.at[slot], f,
                2 * owners[j - 1] + c,
            )
            c_copies[j, n].start()
        part_own[n][...] = total[(Y - 1) * M :]
    loads[7].wait()
    bias = bias_ref[...].reshape(1, -1)
    for n in range(n_chunk):
        cols = slice(int(starts[n]), int(starts[n + 1]))
        total = part_own[n][...]
        for j in range(1, Y):
            c_copies[j, n].wait_recv()
            total = total + part_recv[n][j - 1].astype(F32)
        total = total + bias[:, cols]
        result = (total / (1.0 + jnp.exp(-total))).astype(BF16)
        for t in range(FC):
            for r in range(RD):
                start = t * TD + r * W
                out_ref[r, t, :, cols] = result[start : start + W]

    w_far.wait_send()
    for copy in x_copies + list(c_copies.values()):
        copy.wait_send()

    @pl.when(f < F - 1)
    def _():
        q_copy.wait_send()
        t_copy.wait_send()
        n_copy.wait_send()

    r_copy.wait_send()
    j_copy.wait_send()
    for i, k in t_copies:

        @pl.when(t_sends(i, k))
        def _(i=i, k=k):
            t_copies[i, k].wait_send()

    for k in range(1, down + 1):

        @pl.when(l_sends[k])
        def _(k=k):
            l_copies[k].wait_send()


def per_device(F, H, queries, key_vectors, value_vectors, frame_index, height_index, width_index, frame_block,
               conv_weight, conv_bias):
    FC, HG, W, C = queries.shape
    heads = C // HD
    assert FC == 2 and H % 2 == 0 and F % 2 == 0
    Y = H // 2
    T, TF, RD = FC * HG * W, HG * W, HG // H
    TD = RD * W
    O = conv_weight.shape[-1]
    chunks = [COLUMNS] * (O // COLUMNS) + ([O % COLUMNS] if O % COLUMNS else [])
    steps = max((F // 2 - 1).bit_length(), 1)
    down = (-(-(BLOCK_MOST - 1) // FC) + 1) // 2
    lanes = heads * PAD
    vmem = pl.BlockSpec(memory_space=pltpu.VMEM)
    dma = pltpu.SemaphoreType.DMA
    return pl.pallas_call(
        functools.partial(kernel, (F, Y, heads, HG, W, tuple(chunks))),
        out_shape=jax.ShapeDtypeStruct((RD, FC, W, O), BF16),
        in_specs=[pl.BlockSpec(memory_space=pl.ANY)] * 9,
        out_specs=vmem,
        scratch_shapes=[
            pltpu.VMEM((T, C), BF16),
            pltpu.VMEM((T, C), BF16),
            pltpu.VMEM((T, C), BF16),
            pltpu.SMEM((FC,), jnp.int32),
            pltpu.SMEM((HG,), jnp.int32),
            pltpu.SMEM((W,), jnp.int32),
            pltpu.SMEM((FC,), jnp.int32),
            pltpu.VMEM((O,), F32),
            dma((8,)),
            pltpu.VMEM((2,) + conv_weight.shape, BF16),
            pltpu.VMEM((T, C), BF16),
            pltpu.VMEM((16, lanes), F32),
            pltpu.VMEM((16, lanes), F32),
            pltpu.VMEM((steps, lanes, PAD), BF16),
            *[pltpu.VMEM((lanes, PAD), BF16)] * 4,
            pltpu.VMEM((steps, lanes, PAD), BF16),
            pltpu.VMEM((down, lanes, PAD), BF16),
            *[pltpu.VMEM((lanes, PAD), BF16)] * 3,
            pltpu.VMEM((lanes, PAD), F32),
            pltpu.VMEM((4, lanes, PAD), F32),
            pltpu.VMEM((H, 2 + FC, TD, C), BF16),
            pltpu.VMEM((Y, 2 + FC, TD, C), BF16),
        ]
        + [pltpu.VMEM((max(Y - 1, 1), FC * TD, n), BF16) for n in chunks]
        + [pltpu.VMEM((max(Y - 1, 1), FC * TD, n), BF16) for n in chunks]
        + [pltpu.VMEM((FC * TD, n), F32) for n in chunks]
        + [
            dma, dma, dma, dma((2,)), dma((2,)),
            dma((2**steps,)), dma((steps,)), dma((down,)), dma((down,)), dma((3,)), dma((3,)),
            dma((Y,)), dma((Y,)),
            dma((max(Y - 1, 1) * len(chunks),)), dma((max(Y - 1, 1) * len(chunks),)),
        ],
        compiler_params=pltpu.CompilerParams(
            collective_id=0, has_side_effects=True, vmem_limit_bytes=60 * 1024 * 1024
        ),
        name="attend_conv",
    )(
        queries.reshape(T, C),
        key_vectors.reshape(T, C),
        value_vectors.reshape(T, C),
        frame_index,
        height_index,
        width_index,
        frame_block,
        conv_weight,
        conv_bias,
    )


def solution(mesh):
    placed = (
        P("frame", None, None, "head"),
        P("frame", None, None, "head"),
        P("frame", None, None, "head"),
        P("frame"),
        P(),
        P(),
        P("frame"),
        P(None, "head", None),
        P(),
    )
    return jax.shard_map(
        functools.partial(per_device, mesh.shape["frame"], mesh.shape["head"]),
        mesh=mesh,
        in_specs=placed,
        out_specs=P("head", "frame", None, None),
        check_vma=False,
    )
```

```python
import functools

import jax
import jax.numpy as jnp
import numpy as np
from jax import lax
from jax.experimental import pallas as pl
from jax.experimental.pallas import tpu as pltpu
from jax.sharding import PartitionSpec as P

HD = 112
PAD = 128
EPSILON = 1e-06
BLOCK_MOST = 6
COLUMNS = 512
F32 = jnp.float32
BF16 = jnp.bfloat16


def sections():
    side = HD * 5 // 14 // 2 * 2
    first = HD - 2 * side
    return ((0, first), (first, side), (first + side, side))


def tables(heads):
    C, lanes = heads * HD, heads * PAD
    lane = lax.broadcasted_iota(jnp.int32, (1, lanes), 1)
    head, d = lane // PAD, lane % PAD
    inside = d < HD
    source = jnp.where(inside, head * HD + d, -1)
    partner, sign = jnp.full_like(lane, -1), jnp.zeros((1, lanes), F32)
    freqs, masks = [], []
    for start, n in sections():
        half = n // 2
        low = (d >= start) & (d < start + half)
        high = (d >= start + half) & (d < start + n)
        partner = jnp.where(low, source + half, jnp.where(high, source - half, partner))
        sign = jnp.where(low, -1.0, jnp.where(high, 1.0, sign))
        j = jnp.where(low, d - start, d - start - half).astype(F32)
        either = low | high
        freqs.append(jnp.where(either, jnp.exp(j * float(-2.0 * np.log(10000.0) / n)), 0.0))
        masks.append(jnp.where(either, 1.0, 0.0))
    row = lax.broadcasted_iota(jnp.int32, (C, lanes), 0)
    spread = jnp.where(row == source, 1.0, 0.0).astype(BF16)
    swap = jnp.where(row == partner, sign, 0.0).astype(BF16)
    column = lax.broadcasted_iota(jnp.int32, (1, C), 1)
    target = column // HD * PAD + column % HD
    row = lax.broadcasted_iota(jnp.int32, (lanes, C), 0)
    gather = jnp.where(row == target, 1.0, 0.0).astype(BF16)
    return spread, swap, gather, freqs, masks


def positions(ref, count, rows, lanes):
    row = lax.broadcasted_iota(jnp.int32, (rows, lanes), 0)
    result = jnp.zeros((rows, lanes), F32)
    for i in range(count):
        result = jnp.where(row == i, ref[i].astype(F32), result)
    return result


def mm(a, b):
    return jnp.dot(a, b, preferred_element_type=F32)


def mm_t(a, b):
    return lax.dot_general(a, b, (((0,), (0,)), ((), ())), preferred_element_type=F32)


def mm_n(a, b):
    return lax.dot_general(a, b, (((1,), (1,)), ((), ())), preferred_element_type=F32)


def split(a):
    high = a.astype(BF16)
    return high, (a - high.astype(F32)).astype(BF16)


def kernel(
    cfg, q_any, k_any, v_any, fi_any, hi_any, wi_any, fb_any, w_ref, bias_any, out_ref,
    q_ref, k_ref, v_ref, fi_ref, hi_ref, wi_ref, fb_ref, bias_ref, in_sem, w_buf, qh, time_own, time_prev, msg_t, msg_l, msg_n, msg_r, msg_j, recv_t, recv_l, recv_n, recv_r, recv_j, base, state, att, att_x, *rest,
):
    F, Y, heads, HG, W, chunks = cfg
    n_chunk = len(chunks)
    part_send, part_recv, part_own = rest[:n_chunk], rest[n_chunk : 2 * n_chunk], rest[2 * n_chunk : 3 * n_chunk]
    (w_sem, w_send, w_recv, halo_send, halo_recv, t_send, t_recv, l_send, l_recv, p_send, p_recv,
          x_send, x_recv, c_send, c_recv) = rest[3 * n_chunk :]
    FC = 2
    H = 2 * Y
    TF = HG * W
    RD = HG // H
    TD = RD * W
    O = F // 2
    reach = -(-(BLOCK_MOST - 1) // FC)
    down = (reach + 1) // 2
    f = lax.axis_index("frame")
    h = lax.axis_index("head")
    y, c = h // 2, h % 2
    mate = 2 * y + (1 - c)
    inner, outer = f % 2, f // 2
    partner = f + 1 - 2 * inner

    loads = [
        pltpu.make_async_copy(src, dst, in_sem.at[i])
        for i, (src, dst) in enumerate(
            [(fi_any, fi_ref), (hi_any, hi_ref), (wi_any, wi_ref), (fb_any, fb_ref), (k_any, k_ref), (v_any, v_ref),
             (q_any, q_ref), (bias_any, bias_ref)]
        )
    ]
    for load in loads:
        load.start()

    barrier = pltpu.get_barrier_semaphore()
    for k in range(1, F):
        pl.semaphore_signal(barrier, inc=1, device_id=(lax.rem(f + k, F), h), device_id_type=pl.DeviceIdType.MESH)
    pl.semaphore_signal(barrier, inc=1, device_id=(f, mate), device_id_type=pl.DeviceIdType.MESH)
    for j in range(1, Y):
        pl.semaphore_signal(
            barrier, inc=1, device_id=(f, 2 * lax.rem(y + j, Y) + c), device_id_type=pl.DeviceIdType.MESH
        )

    def remote(src, dst, send, recv, frame, head):
        return pltpu.make_async_remote_copy(
            src_ref=src, dst_ref=dst, send_sem=send, recv_sem=recv,
            device_id=(frame, head), device_id_type=pl.DeviceIdType.MESH,
        )

    w_local = pltpu.make_async_copy(w_ref, w_buf.at[0], w_sem)
    w_local.start()

    pl.semaphore_wait(barrier, (F - 1) + 1 + (Y - 1))

    w_far = remote(w_ref, w_buf.at[1], w_send, w_recv, f, mate)
    nxt = lax.rem(f + 1, F)
    q_copy = remote(q_any, qh, halo_send.at[0], halo_recv.at[0], nxt, h)
    t_copy = remote(time_own, time_prev, halo_send.at[1], halo_recv.at[1], nxt, h)

    @pl.when(f < F - 1)
    def _():
        q_copy.start()

    lanes = heads * PAD
    spread, swap, gather, freqs, masks = tables(heads)
    for load in loads[:4]:
        load.wait()
    t_ang = positions(fi_ref, FC, 8, lanes) * freqs[0]
    time_own[0:8, :] = jnp.cos(t_ang) * masks[0]
    time_own[8:16, :] = jnp.sin(t_ang)
    h_ang = positions(hi_ref, HG, HG, lanes) * freqs[1]
    w_ang = positions(wi_ref, W, W, lanes) * freqs[2]
    cos_hw = (
        (jnp.cos(h_ang) * masks[1]).reshape(HG, 1, lanes) + (jnp.cos(w_ang) * masks[2]).reshape(1, W, lanes)
    ).reshape(TF, lanes)
    sin_hw = (jnp.sin(h_ang).reshape(HG, 1, lanes) + jnp.sin(w_ang).reshape(1, W, lanes)).reshape(TF, lanes)

    @pl.when(f < F - 1)
    def _():
        t_copy.start()

    @pl.when(f == 0)
    def _():
        qh[...] = jnp.zeros_like(qh)
        time_prev[...] = jnp.zeros_like(time_prev)
        recv_n[...] = jnp.zeros_like(recv_n)


    def rotated(rows, cos_t, sin_t):
        positive = jnp.maximum(rows, jnp.zeros_like(rows))
        plain = mm(positive, spread)
        turned = mm(positive, swap)
        return plain.astype(BF16), plain * (cos_hw + cos_t) + turned * (sin_hw + sin_t)

    ones = jnp.where(lax.broadcasted_iota(jnp.int32, (PAD, TF), 0) >= HD, 1.0, 0.0).astype(BF16)
    for load in loads[4:6]:
        load.wait()
    frames = []
    for t in range(FC):
        rows = slice(t * TF, (t + 1) * TF)
        k_pos, k_rot = rotated(k_ref[rows, :], time_own[t : t + 1, :], time_own[8 + t : 9 + t, :])
        k_hi, k_lo = split(k_rot)
        value = mm(v_ref[rows, :], spread).astype(BF16)
        per_head = []
        totals = mm(ones, k_pos)
        for g in range(heads):
            cut = slice(g * PAD, (g + 1) * PAD)
            both = mm_t(value[:, cut], jnp.concatenate([k_hi[:, cut], k_lo[:, cut]], axis=1))
            per_head.append(both[:, :PAD] + both[:, PAD:] + totals[:, cut])
        frames.append(jnp.concatenate(per_head, axis=0))
    id0 = fb_ref[0].astype(F32)
    id1 = fb_ref[1].astype(F32)
    same = jnp.where(id0 == id1, 1.0, 0.0)
    own_t = frames[0] + frames[1]
    own_l = frames[0] + same * frames[1]
    row = lax.broadcasted_iota(jnp.int32, own_t.shape, 0)

    def tagged(value, first, second):
        return jnp.where(row == HD + 1, first, jnp.where(row == HD + 2, second, value)).astype(BF16)

    msg_t[0] = own_t.astype(BF16)
    msg_l[...] = tagged(own_l, id0, id1)
    msg_n[...] = tagged((same - 1.0) * frames[1], id0, id1)

    t_copies, l_copies, l_sends, l_gets = {}, {}, {}, {}
    steps = (O - 1).bit_length()
    for i in range(steps):
        for k in range(1, 2**i + 1):
            t_copies[i, k] = remote(
                msg_t.at[i], recv_t.at[i], t_send.at[2**i + k - 2], t_recv.at[i], lax.rem(f + 2 * k, F), h
            )

    def t_sends(i, k):
        return (outer % 2 ** (i + 1) == 2**i - 1) & (outer + k < O)

    def t_start(i):
        for k in range(2**i, 0, -1):

            @pl.when(t_sends(i, k))
            def _(k=k):
                t_copies[i, k].start()

    for k in range(1, down + 1):
        l_copies[k] = remote(
            msg_l, recv_l.at[k - 1], l_send.at[k - 1], l_recv.at[k - 1], lax.rem(f - 2 * k + 2 * F, F), h
        )
        wanted = 2 * k <= reach + 1 - inner
        l_sends[k] = wanted & (outer >= k)
        l_gets[k] = wanted & (outer + k < O)
    n_copy = remote(msg_n, recv_n, p_send.at[0], p_recv.at[0], nxt, h)
    r_copy = remote(msg_r, recv_r, p_send.at[1], p_recv.at[1], partner, h)
    j_copy = remote(msg_j, recv_j, p_send.at[2], p_recv.at[2], partner, h)
    @pl.when(f < F - 1)
    def _():
        n_copy.start()

    t_start(0)

    for k in range(down, 0, -1):

        @pl.when(l_sends[k])
        def _(k=k):
            l_copies[k].start()

    w_far.start()

    base[...] = jnp.zeros_like(own_t)
    for i in range(steps):

        @pl.when(outer // 2**i % 2 == 1)
        def _(i=i):
            t_copies[i, 1].wait_recv()
            base[...] += recv_t[i].astype(F32)

        if i + 1 < steps:
            msg_t[i + 1] = (base[...] + own_t).astype(BF16)
            t_start(i + 1)

    earlier = base[...]
    msg_r[...] = (earlier + jnp.where(inner == 0, 1.0, 0.0) * own_t).astype(BF16)
    r_copy.start()

    for k in range(1, down + 1):

        @pl.when(l_gets[k])
        def _(k=k):
            l_copies[k].wait_recv()

        @pl.when(jnp.logical_not(l_gets[k]))
        def _(k=k):
            recv_l[k - 1] = tagged(jnp.zeros_like(own_t), -1.0, -1.0)

    def joined(ident, total, pieces):
        for piece in pieces:
            total = total + jnp.where(piece[HD + 1 : HD + 2] == ident, 1.0, 0.0) * piece
        return tagged(total, ident, ident)

    leads = [recv_l[k].astype(F32) for k in range(down)]

    @pl.when(inner == 0)
    def _():
        msg_j[...] = joined(leads[0][HD + 1 : HD + 2], leads[0], leads[1:])

    @pl.when(inner == 1)
    def _():
        msg_j[...] = joined(id0, own_l, leads[:1])

    j_copy.start()

    loads[6].wait()
    q_parts = [None, None]
    for t in range(FC):
        rows = slice(t * TF, (t + 1) * TF)
        q_parts.append(rotated(q_ref[rows, :], time_own[t : t + 1, :], time_own[8 + t : 9 + t, :]))

    @pl.when(f > 0)
    def _():
        q_copy.wait_recv()
        t_copy.wait_recv()

    for t in range(FC):
        rows = slice(t * TF, (t + 1) * TF)
        q_parts[t] = rotated(qh[rows, :], time_prev[t : t + 1, :], time_prev[8 + t : 9 + t, :])

    @pl.when(f > 0)
    def _():
        n_copy.wait_recv()

    r_copy.wait_recv()
    j_copy.wait_recv()
    before = earlier + recv_r[...].astype(F32)
    less = recv_n[...].astype(F32)
    tails = [recv_j[...].astype(F32)] + leads
    ids = [less[HD + 1 : HD + 2], less[HD + 2 : HD + 3], id0, id1]
    starts = [before + less, before, before + own_l, before + own_t]
    for i in range(2 + FC):
        total = starts[i]
        if i < 2:
            total = total + jnp.where(ids[i] == id0, 1.0, 0.0) * own_l
        for tail in tails:
            total = total + jnp.where(tail[HD + 1 : HD + 2] == ids[i], 1.0, 0.0) * tail
        state[i] = total

    for t in range(2 + FC):
        q_pos, q_rot = q_parts[t]
        q_hi, q_lo = split(q_rot)
        full = state[t]
        merged = []
        for g in range(heads):
            cut = slice(g * PAD, (g + 1) * PAD)
            block = full[cut, :]
            s_hi, s_lo = split(block)
            total_hi, total_lo = split(jnp.broadcast_to(block[HD : HD + 1, :], (PAD, PAD)))
            both = mm_n(q_hi[:, cut], jnp.concatenate([s_hi, s_lo], axis=0))
            numerator = both[:, :PAD] + both[:, PAD:] + mm_n(q_lo[:, cut], s_hi)
            both = mm_n(q_pos[:, cut], jnp.concatenate([total_hi, total_lo], axis=0))
            denominator = both[:, :PAD] + both[:, PAD:] + EPSILON
            merged.append((numerator / denominator).astype(BF16))
        tight = mm(jnp.concatenate(merged, axis=1), gather).astype(BF16)
        for g in range(H):
            att[g, t] = tight[g * TD : (g + 1) * TD]

    x_copies = []
    for j in range(Y):
        x_copies.append(remote(att.at[2 * j + 1 - c], att_x.at[j], x_send.at[j], x_recv.at[j], f, mate))
        x_copies[-1].start()
    w_local.wait()
    w_far.wait_recv()
    for copy in x_copies:
        copy.wait_recv()

    starts = np.cumsum([0] + list(chunks))
    owners = [lax.rem(y + j, Y) for j in range(1, Y)] + [y]
    M = FC * TD
    taps = []
    for tap in range(3):
        for side in range(2):
            rows = [(att.at[2 * j + c] if side == 0 else att_x.at[j])[2 - tap : 2 - tap + FC] for j in owners]
            taps.append((tap, side, jnp.concatenate([r.reshape(M, heads * HD) for r in rows], axis=0)))

    c_copies = {}
    for n in range(n_chunk):
        cols = slice(int(starts[n]), int(starts[n + 1]))
        total = None
        for tap, side, rows in taps:
            term = mm(rows, w_buf[side, tap, :, cols])
            total = term if total is None else total + term
        for j in range(1, Y):
            part_send[n][j - 1] = total[(j - 1) * M : j * M].astype(BF16)
            slot = (j - 1) * n_chunk + n
            c_copies[j, n] = remote(
                part_send[n].at[j - 1], part_recv[n].at[j - 1], c_send.at[slot], c_recv.at[slot], f,
                2 * owners[j - 1] + c,
            )
            c_copies[j, n].start()
        part_own[n][...] = total[(Y - 1) * M :]
    loads[7].wait()
    bias = bias_ref[...].reshape(1, -1)
    for n in range(n_chunk):
        cols = slice(int(starts[n]), int(starts[n + 1]))
        total = part_own[n][...]
        for j in range(1, Y):
            c_copies[j, n].wait_recv()
            total = total + part_recv[n][j - 1].astype(F32)
        total = total + bias[:, cols]
        result = (total / (1.0 + jnp.exp(-total))).astype(BF16)
        for t in range(FC):
            for r in range(RD):
                start = t * TD + r * W
                out_ref[r, t, :, cols] = result[start : start + W]

    w_far.wait_send()
    for copy in x_copies + list(c_copies.values()):
        copy.wait_send()

    @pl.when(f < F - 1)
    def _():
        q_copy.wait_send()
        t_copy.wait_send()
        n_copy.wait_send()

    r_copy.wait_send()
    j_copy.wait_send()
    for i, k in t_copies:

        @pl.when(t_sends(i, k))
        def _(i=i, k=k):
            t_copies[i, k].wait_send()

    for k in range(1, down + 1):

        @pl.when(l_sends[k])
        def _(k=k):
            l_copies[k].wait_send()


def per_device(F, H, queries, key_vectors, value_vectors, frame_index, height_index, width_index, frame_block,
               conv_weight, conv_bias):
    FC, HG, W, C = queries.shape
    heads = C // HD
    assert FC == 2 and H % 2 == 0 and F % 2 == 0
    Y = H // 2
    T, TF, RD = FC * HG * W, HG * W, HG // H
    TD = RD * W
    O = conv_weight.shape[-1]
    chunks = [COLUMNS] * (O // COLUMNS) + ([O % COLUMNS] if O % COLUMNS else [])
    steps = max((F // 2 - 1).bit_length(), 1)
    down = (-(-(BLOCK_MOST - 1) // FC) + 1) // 2
    lanes = heads * PAD
    vmem = pl.BlockSpec(memory_space=pltpu.VMEM)
    dma = pltpu.SemaphoreType.DMA
    return pl.pallas_call(
        functools.partial(kernel, (F, Y, heads, HG, W, tuple(chunks))),
        out_shape=jax.ShapeDtypeStruct((RD, FC, W, O), BF16),
        in_specs=[pl.BlockSpec(memory_space=pl.ANY)] * 9,
        out_specs=vmem,
        scratch_shapes=[
            pltpu.VMEM((T, C), BF16),
            pltpu.VMEM((T, C), BF16),
            pltpu.VMEM((T, C), BF16),
            pltpu.SMEM((FC,), jnp.int32),
            pltpu.SMEM((HG,), jnp.int32),
            pltpu.SMEM((W,), jnp.int32),
            pltpu.SMEM((FC,), jnp.int32),
            pltpu.VMEM((O,), F32),
            dma((8,)),
            pltpu.VMEM((2,) + conv_weight.shape, BF16),
            pltpu.VMEM((T, C), BF16),
            pltpu.VMEM((16, lanes), F32),
            pltpu.VMEM((16, lanes), F32),
            pltpu.VMEM((steps, lanes, PAD), BF16),
            *[pltpu.VMEM((lanes, PAD), BF16)] * 4,
            pltpu.VMEM((steps, lanes, PAD), BF16),
            pltpu.VMEM((down, lanes, PAD), BF16),
            *[pltpu.VMEM((lanes, PAD), BF16)] * 3,
            pltpu.VMEM((lanes, PAD), F32),
            pltpu.VMEM((4, lanes, PAD), F32),
            pltpu.VMEM((H, 2 + FC, TD, C), BF16),
            pltpu.VMEM((Y, 2 + FC, TD, C), BF16),
        ]
        + [pltpu.VMEM((max(Y - 1, 1), FC * TD, n), BF16) for n in chunks]
        + [pltpu.VMEM((max(Y - 1, 1), FC * TD, n), BF16) for n in chunks]
        + [pltpu.VMEM((FC * TD, n), F32) for n in chunks]
        + [
            dma, dma, dma, dma((2,)), dma((2,)),
            dma((2**steps,)), dma((steps,)), dma((down,)), dma((down,)), dma((3,)), dma((3,)),
            dma((Y,)), dma((Y,)),
            dma((max(Y - 1, 1) * len(chunks),)), dma((max(Y - 1, 1) * len(chunks),)),
        ],
        compiler_params=pltpu.CompilerParams(
            collective_id=0, has_side_effects=True, vmem_limit_bytes=60 * 1024 * 1024
        ),
        name="attend_conv",
    )(
        queries.reshape(T, C),
        key_vectors.reshape(T, C),
        value_vectors.reshape(T, C),
        frame_index,
        height_index,
        width_index,
        frame_block,
        conv_weight,
        conv_bias,
    )


def solution(mesh):
    placed = (
        P("frame", None, None, "head"),
        P("frame", None, None, "head"),
        P("frame", None, None, "head"),
        P("frame"),
        P(),
        P(),
        P("frame"),
        P(None, "head", None),
        P(),
    )
    return jax.shard_map(
        functools.partial(per_device, mesh.shape["frame"], mesh.shape["head"]),
        mesh=mesh,
        in_specs=placed,
        out_specs=P("head", "frame", None, None),
        check_vma=False,
    )
```

```python
import functools

import jax
import jax.numpy as jnp
import numpy as np
from jax import lax
from jax.experimental import pallas as pl
from jax.experimental.pallas import tpu as pltpu
from jax.sharding import PartitionSpec as P

HD = 112
PAD = 128
EPSILON = 1e-06
BLOCK_MOST = 6
COLUMNS = 512
F32 = jnp.float32
BF16 = jnp.bfloat16


def sections():
    side = HD * 5 // 14 // 2 * 2
    first = HD - 2 * side
    return ((0, first), (first, side), (first + side, side))


def tables(heads):
    C, lanes = heads * HD, heads * PAD
    lane = lax.broadcasted_iota(jnp.int32, (1, lanes), 1)
    head, d = lane // PAD, lane % PAD
    inside = d < HD
    source = jnp.where(inside, head * HD + d, -1)
    partner, sign = jnp.full_like(lane, -1), jnp.zeros((1, lanes), F32)
    freqs, masks = [], []
    for start, n in sections():
        half = n // 2
        low = (d >= start) & (d < start + half)
        high = (d >= start + half) & (d < start + n)
        partner = jnp.where(low, source + half, jnp.where(high, source - half, partner))
        sign = jnp.where(low, -1.0, jnp.where(high, 1.0, sign))
        j = jnp.where(low, d - start, d - start - half).astype(F32)
        either = low | high
        freqs.append(jnp.where(either, jnp.exp(j * float(-2.0 * np.log(10000.0) / n)), 0.0))
        masks.append(jnp.where(either, 1.0, 0.0))
    row = lax.broadcasted_iota(jnp.int32, (C, lanes), 0)
    spread = jnp.where(row == source, 1.0, 0.0).astype(BF16)
    swap = jnp.where(row == partner, sign, 0.0).astype(BF16)
    column = lax.broadcasted_iota(jnp.int32, (1, C), 1)
    target = column // HD * PAD + column % HD
    row = lax.broadcasted_iota(jnp.int32, (lanes, C), 0)
    gather = jnp.where(row == target, 1.0, 0.0).astype(BF16)
    return spread, swap, gather, freqs, masks


def positions(ref, count, rows, lanes):
    row = lax.broadcasted_iota(jnp.int32, (rows, lanes), 0)
    result = jnp.zeros((rows, lanes), F32)
    for i in range(count):
        result = jnp.where(row == i, ref[i].astype(F32), result)
    return result


def mm(a, b):
    return jnp.dot(a, b, preferred_element_type=F32)


def mm_t(a, b):
    return lax.dot_general(a, b, (((0,), (0,)), ((), ())), preferred_element_type=F32)


def mm_n(a, b):
    return lax.dot_general(a, b, (((1,), (1,)), ((), ())), preferred_element_type=F32)


def split(a):
    high = a.astype(BF16)
    return high, (a - high.astype(F32)).astype(BF16)


def kernel(
    cfg, q_any, k_any, v_any, fi_any, hi_any, wi_any, fb_any, w_ref, bias_any, out_ref,
    q_ref, k_ref, v_ref, fi_ref, hi_ref, wi_ref, fb_ref, bias_ref, in_sem, w_buf, qh, time_own, time_prev, msg_t, msg_l, msg_n, msg_r, msg_j, recv_t, recv_l, recv_n, recv_r, recv_j, base, state, att, att_x, *rest,
):
    F, Y, heads, HG, W, chunks = cfg
    n_chunk = len(chunks)
    part_send, part_recv, part_own = rest[:n_chunk], rest[n_chunk : 2 * n_chunk], rest[2 * n_chunk : 3 * n_chunk]
    (w_sem, w_send, w_recv, halo_send, halo_recv, t_send, t_recv, l_send, l_recv, p_send, p_recv,
          x_send, x_recv, c_send, c_recv) = rest[3 * n_chunk :]
    FC = 2
    H = 2 * Y
    TF = HG * W
    RD = HG // H
    TD = RD * W
    O = F // 2
    reach = -(-(BLOCK_MOST - 1) // FC)
    down = (reach + 1) // 2
    f = lax.axis_index("frame")
    h = lax.axis_index("head")
    y, c = h // 2, h % 2
    mate = 2 * y + (1 - c)
    inner, outer = f % 2, f // 2
    partner = f + 1 - 2 * inner

    loads = [
        pltpu.make_async_copy(src, dst, in_sem.at[i])
        for i, (src, dst) in enumerate(
            [(fi_any, fi_ref), (hi_any, hi_ref), (wi_any, wi_ref), (fb_any, fb_ref), (k_any, k_ref), (v_any, v_ref),
             (q_any, q_ref), (bias_any, bias_ref)]
        )
    ]
    for load in loads:
        load.start()

    barrier = pltpu.get_barrier_semaphore()
    for k in range(1, F):
        pl.semaphore_signal(barrier, inc=1, device_id=(lax.rem(f + k, F), h), device_id_type=pl.DeviceIdType.MESH)
    pl.semaphore_signal(barrier, inc=1, device_id=(f, mate), device_id_type=pl.DeviceIdType.MESH)
    for j in range(1, Y):
        pl.semaphore_signal(
            barrier, inc=1, device_id=(f, 2 * lax.rem(y + j, Y) + c), device_id_type=pl.DeviceIdType.MESH
        )

    def remote(src, dst, send, recv, frame, head):
        return pltpu.make_async_remote_copy(
            src_ref=src, dst_ref=dst, send_sem=send, recv_sem=recv,
            device_id=(frame, head), device_id_type=pl.DeviceIdType.MESH,
        )

    w_local = pltpu.make_async_copy(w_ref, w_buf.at[0], w_sem)
    w_local.start()

    pl.semaphore_wait(barrier, (F - 1) + 1 + (Y - 1))

    w_far = remote(w_ref, w_buf.at[1], w_send, w_recv, f, mate)
    nxt = lax.rem(f + 1, F)
    q_copy = remote(q_any, qh, halo_send.at[0], halo_recv.at[0], nxt, h)
    t_copy = remote(time_own, time_prev, halo_send.at[1], halo_recv.at[1], nxt, h)

    @pl.when(f < F - 1)
    def _():
        q_copy.start()

    lanes = heads * PAD
    spread, swap, gather, freqs, masks = tables(heads)
    for load in loads[:4]:
        load.wait()
    t_ang = positions(fi_ref, FC, 8, lanes) * freqs[0]
    time_own[0:8, :] = jnp.cos(t_ang) * masks[0]
    time_own[8:16, :] = jnp.sin(t_ang)
    h_ang = positions(hi_ref, HG, HG, lanes) * freqs[1]
    w_ang = positions(wi_ref, W, W, lanes) * freqs[2]
    cos_hw = (
        (jnp.cos(h_ang) * masks[1]).reshape(HG, 1, lanes) + (jnp.cos(w_ang) * masks[2]).reshape(1, W, lanes)
    ).reshape(TF, lanes)
    sin_hw = (jnp.sin(h_ang).reshape(HG, 1, lanes) + jnp.sin(w_ang).reshape(1, W, lanes)).reshape(TF, lanes)

    @pl.when(f < F - 1)
    def _():
        t_copy.start()

    @pl.when(f == 0)
    def _():
        qh[...] = jnp.zeros_like(qh)
        time_prev[...] = jnp.zeros_like(time_prev)
        recv_n[...] = jnp.zeros_like(recv_n)


    def rotated(rows, cos_t, sin_t):
        positive = jnp.maximum(rows, jnp.zeros_like(rows))
        plain = mm(positive, spread)
        turned = mm(positive, swap)
        return plain.astype(BF16), plain * (cos_hw + cos_t) + turned * (sin_hw + sin_t)

    ones = jnp.where(lax.broadcasted_iota(jnp.int32, (PAD, TF), 0) >= HD, 1.0, 0.0).astype(BF16)
    for load in loads[4:6]:
        load.wait()
    frames = []
    for t in range(FC):
        rows = slice(t * TF, (t + 1) * TF)
        k_pos, k_rot = rotated(k_ref[rows, :], time_own[t : t + 1, :], time_own[8 + t : 9 + t, :])
        k_hi, k_lo = split(k_rot)
        value = mm(v_ref[rows, :], spread).astype(BF16)
        per_head = []
        totals = mm(ones, k_pos)
        for g in range(heads):
            cut = slice(g * PAD, (g + 1) * PAD)
            both = mm_t(value[:, cut], jnp.concatenate([k_hi[:, cut], k_lo[:, cut]], axis=1))
            per_head.append(both[:, :PAD] + both[:, PAD:] + totals[:, cut])
        frames.append(jnp.concatenate(per_head, axis=0))
    id0 = fb_ref[0].astype(F32)
    id1 = fb_ref[1].astype(F32)
    same = jnp.where(id0 == id1, 1.0, 0.0)
    own_t = frames[0] + frames[1]
    own_l = frames[0] + same * frames[1]
    row = lax.broadcasted_iota(jnp.int32, own_t.shape, 0)

    def tagged(value, first, second):
        return jnp.where(row == HD + 1, first, jnp.where(row == HD + 2, second, value)).astype(BF16)

    msg_t[...] = own_t.astype(BF16)
    msg_l[...] = tagged(own_l, id0, id1)
    msg_n[...] = tagged((same - 1.0) * frames[1], id0, id1)

    t_copies, l_copies, l_sends, l_gets = {}, {}, {}, {}
    for k in range(1, O):
        t_copies[k] = remote(
            msg_t, recv_t.at[k - 1], t_send.at[k - 1], t_recv.at[k - 1], lax.rem(f + 2 * k, F), h
        )
    for k in range(1, down + 1):
        l_copies[k] = remote(
            msg_l, recv_l.at[k - 1], l_send.at[k - 1], l_recv.at[k - 1], lax.rem(f - 2 * k + 2 * F, F), h
        )
        wanted = 2 * k <= reach + 1 - inner
        l_sends[k] = wanted & (outer >= k)
        l_gets[k] = wanted & (outer + k < O)
    n_copy = remote(msg_n, recv_n, p_send.at[0], p_recv.at[0], nxt, h)
    r_copy = remote(msg_r, recv_r, p_send.at[1], p_recv.at[1], partner, h)
    j_copy = remote(msg_j, recv_j, p_send.at[2], p_recv.at[2], partner, h)
    @pl.when(f < F - 1)
    def _():
        n_copy.start()

    for k in range(O - 1, 0, -1):

        @pl.when(outer + k < O)
        def _(k=k):
            t_copies[k].start()

    for k in range(down, 0, -1):

        @pl.when(l_sends[k])
        def _(k=k):
            l_copies[k].start()

    w_far.start()

    @pl.when(inner == 0)
    def _():
        base[...] = own_t

    @pl.when(inner == 1)
    def _():
        base[...] = jnp.zeros_like(own_t)

    for k in range(1, O):

        @pl.when(outer >= k)
        def _(k=k):
            t_copies[k].wait_recv()
            base[...] += recv_t[k - 1].astype(F32)

    msg_r[...] = base[...].astype(BF16)
    r_copy.start()

    for k in range(1, down + 1):

        @pl.when(l_gets[k])
        def _(k=k):
            l_copies[k].wait_recv()

        @pl.when(jnp.logical_not(l_gets[k]))
        def _(k=k):
            recv_l[k - 1] = tagged(jnp.zeros_like(own_t), -1.0, -1.0)

    def joined(ident, total, pieces):
        for piece in pieces:
            total = total + jnp.where(piece[HD + 1 : HD + 2] == ident, 1.0, 0.0) * piece
        return tagged(total, ident, ident)

    leads = [recv_l[k].astype(F32) for k in range(down)]

    @pl.when(inner == 0)
    def _():
        msg_j[...] = joined(leads[0][HD + 1 : HD + 2], leads[0], leads[1:])

    @pl.when(inner == 1)
    def _():
        msg_j[...] = joined(id0, own_l, leads[:1])

    j_copy.start()

    loads[6].wait()
    q_parts = [None, None]
    for t in range(FC):
        rows = slice(t * TF, (t + 1) * TF)
        q_parts.append(rotated(q_ref[rows, :], time_own[t : t + 1, :], time_own[8 + t : 9 + t, :]))

    @pl.when(f > 0)
    def _():
        q_copy.wait_recv()
        t_copy.wait_recv()

    for t in range(FC):
        rows = slice(t * TF, (t + 1) * TF)
        q_parts[t] = rotated(qh[rows, :], time_prev[t : t + 1, :], time_prev[8 + t : 9 + t, :])

    @pl.when(f > 0)
    def _():
        n_copy.wait_recv()

    r_copy.wait_recv()
    j_copy.wait_recv()
    before = base[...] + recv_r[...].astype(F32) - jnp.where(inner == 0, 1.0, 0.0) * own_t
    less = recv_n[...].astype(F32)
    tails = [recv_j[...].astype(F32)] + leads
    ids = [less[HD + 1 : HD + 2], less[HD + 2 : HD + 3], id0, id1]
    starts = [before + less, before, before + own_l, before + own_t]
    for i in range(2 + FC):
        total = starts[i]
        if i < 2:
            total = total + jnp.where(ids[i] == id0, 1.0, 0.0) * own_l
        for tail in tails:
            total = total + jnp.where(tail[HD + 1 : HD + 2] == ids[i], 1.0, 0.0) * tail
        state[i] = total

    for t in range(2 + FC):
        q_pos, q_rot = q_parts[t]
        q_hi, q_lo = split(q_rot)
        full = state[t]
        merged = []
        for g in range(heads):
            cut = slice(g * PAD, (g + 1) * PAD)
            block = full[cut, :]
            s_hi, s_lo = split(block)
            total_hi, total_lo = split(jnp.broadcast_to(block[HD : HD + 1, :], (PAD, PAD)))
            both = mm_n(q_hi[:, cut], jnp.concatenate([s_hi, s_lo], axis=0))
            numerator = both[:, :PAD] + both[:, PAD:] + mm_n(q_lo[:, cut], s_hi)
            both = mm_n(q_pos[:, cut], jnp.concatenate([total_hi, total_lo], axis=0))
            denominator = both[:, :PAD] + both[:, PAD:] + EPSILON
            merged.append((numerator / denominator).astype(BF16))
        tight = mm(jnp.concatenate(merged, axis=1), gather).astype(BF16)
        for g in range(H):
            att[g, t] = tight[g * TD : (g + 1) * TD]

    x_copies = []
    for j in range(Y):
        x_copies.append(remote(att.at[2 * j + 1 - c], att_x.at[j], x_send.at[j], x_recv.at[j], f, mate))
        x_copies[-1].start()
    w_local.wait()
    w_far.wait_recv()
    for copy in x_copies:
        copy.wait_recv()

    starts = np.cumsum([0] + list(chunks))
    owners = [lax.rem(y + j, Y) for j in range(1, Y)] + [y]
    M = FC * TD
    taps = []
    for tap in range(3):
        for side in range(2):
            rows = [(att.at[2 * j + c] if side == 0 else att_x.at[j])[2 - tap : 2 - tap + FC] for j in owners]
            taps.append((tap, side, jnp.concatenate([r.reshape(M, heads * HD) for r in rows], axis=0)))

    c_copies = {}
    for n in range(n_chunk):
        cols = slice(int(starts[n]), int(starts[n + 1]))
        total = None
        for tap, side, rows in taps:
            term = mm(rows, w_buf[side, tap, :, cols])
            total = term if total is None else total + term
        for j in range(1, Y):
            part_send[n][j - 1] = total[(j - 1) * M : j * M].astype(BF16)
            slot = (j - 1) * n_chunk + n
            c_copies[j, n] = remote(
                part_send[n].at[j - 1], part_recv[n].at[j - 1], c_send.at[slot], c_recv.at[slot], f,
                2 * owners[j - 1] + c,
            )
            c_copies[j, n].start()
        part_own[n][...] = total[(Y - 1) * M :]
    loads[7].wait()
    bias = bias_ref[...].reshape(1, -1)
    for n in range(n_chunk):
        cols = slice(int(starts[n]), int(starts[n + 1]))
        total = part_own[n][...]
        for j in range(1, Y):
            c_copies[j, n].wait_recv()
            total = total + part_recv[n][j - 1].astype(F32)
        total = total + bias[:, cols]
        result = (total / (1.0 + jnp.exp(-total))).astype(BF16)
        for t in range(FC):
            for r in range(RD):
                start = t * TD + r * W
                out_ref[r, t, :, cols] = result[start : start + W]

    w_far.wait_send()
    for copy in x_copies + list(c_copies.values()):
        copy.wait_send()

    @pl.when(f < F - 1)
    def _():
        q_copy.wait_send()
        t_copy.wait_send()
        n_copy.wait_send()

    r_copy.wait_send()
    j_copy.wait_send()
    for k in range(1, O):

        @pl.when(outer + k < O)
        def _(k=k):
            t_copies[k].wait_send()

    for k in range(1, down + 1):

        @pl.when(l_sends[k])
        def _(k=k):
            l_copies[k].wait_send()


def per_device(F, H, queries, key_vectors, value_vectors, frame_index, height_index, width_index, frame_block,
               conv_weight, conv_bias):
    FC, HG, W, C = queries.shape
    heads = C // HD
    assert FC == 2 and H % 2 == 0 and F % 2 == 0
    Y = H // 2
    T, TF, RD = FC * HG * W, HG * W, HG // H
    TD = RD * W
    O = conv_weight.shape[-1]
    chunks = [COLUMNS] * (O // COLUMNS) + ([O % COLUMNS] if O % COLUMNS else [])
    outer = max(F // 2 - 1, 1)
    down = (-(-(BLOCK_MOST - 1) // FC) + 1) // 2
    lanes = heads * PAD
    vmem = pl.BlockSpec(memory_space=pltpu.VMEM)
    dma = pltpu.SemaphoreType.DMA
    return pl.pallas_call(
        functools.partial(kernel, (F, Y, heads, HG, W, tuple(chunks))),
        out_shape=jax.ShapeDtypeStruct((RD, FC, W, O), BF16),
        in_specs=[pl.BlockSpec(memory_space=pl.ANY)] * 9,
        out_specs=vmem,
        scratch_shapes=[
            pltpu.VMEM((T, C), BF16),
            pltpu.VMEM((T, C), BF16),
            pltpu.VMEM((T, C), BF16),
            pltpu.SMEM((FC,), jnp.int32),
            pltpu.SMEM((HG,), jnp.int32),
            pltpu.SMEM((W,), jnp.int32),
            pltpu.SMEM((FC,), jnp.int32),
            pltpu.VMEM((O,), F32),
            dma((8,)),
            pltpu.VMEM((2,) + conv_weight.shape, BF16),
            pltpu.VMEM((T, C), BF16),
            pltpu.VMEM((16, lanes), F32),
            pltpu.VMEM((16, lanes), F32),
            *[pltpu.VMEM((lanes, PAD), BF16)] * 5,
            pltpu.VMEM((outer, lanes, PAD), BF16),
            pltpu.VMEM((down, lanes, PAD), BF16),
            *[pltpu.VMEM((lanes, PAD), BF16)] * 3,
            pltpu.VMEM((lanes, PAD), F32),
            pltpu.VMEM((4, lanes, PAD), F32),
            pltpu.VMEM((H, 2 + FC, TD, C), BF16),
            pltpu.VMEM((Y, 2 + FC, TD, C), BF16),
        ]
        + [pltpu.VMEM((max(Y - 1, 1), FC * TD, n), BF16) for n in chunks]
        + [pltpu.VMEM((max(Y - 1, 1), FC * TD, n), BF16) for n in chunks]
        + [pltpu.VMEM((FC * TD, n), F32) for n in chunks]
        + [
            dma, dma, dma, dma((2,)), dma((2,)),
            dma((outer,)), dma((outer,)), dma((down,)), dma((down,)), dma((3,)), dma((3,)),
            dma((Y,)), dma((Y,)),
            dma((max(Y - 1, 1) * len(chunks),)), dma((max(Y - 1, 1) * len(chunks),)),
        ],
        compiler_params=pltpu.CompilerParams(
            collective_id=0, has_side_effects=True, vmem_limit_bytes=60 * 1024 * 1024
        ),
        name="attend_conv",
    )(
        queries.reshape(T, C),
        key_vectors.reshape(T, C),
        value_vectors.reshape(T, C),
        frame_index,
        height_index,
        width_index,
        frame_block,
        conv_weight,
        conv_bias,
    )


def solution(mesh):
    placed = (
        P("frame", None, None, "head"),
        P("frame", None, None, "head"),
        P("frame", None, None, "head"),
        P("frame"),
        P(),
        P(),
        P("frame"),
        P(None, "head", None),
        P(),
    )
    return jax.shard_map(
        functools.partial(per_device, mesh.shape["frame"], mesh.shape["head"]),
        mesh=mesh,
        in_specs=placed,
        out_specs=P("head", "frame", None, None),
        check_vma=False,
    )
```
